128 devices in a mesh: row: 8 (over y_lo, z), col: 16 (over y_hi, x, core).
Axes of the slice: x: 4, y: 4 (y_hi: 2, y_lo: 2; y = y_hi * 2 + y_lo), z: 4, core: 2. Of those that a mesh axis runs over, the one named last changes fastest.
Arguments:
- pair: float32 [512, 512, 128], P('row', 'col'), may hold values from -6 to 6
- chain_lengths: int32 [8], replicated, may hold values from 1 to 64, 384 in all
- tri_in: bfloat16 [128, 640], replicated, may hold values from -0.5 to 0.5
- tri_out: bfloat16 [128, 128], replicated, may hold values from -0.5 to 0.5
- att_in: bfloat16 [128, 512], replicated, may hold values from -0.5 to 0.5
- att_bias: float32 [128, 4], replicated, may hold values from -6 to 6
- att_out: bfloat16 [128, 128], replicated, may hold values from -0.5 to 0.5
Outputs:
- pair_out: float32 [512, 512, 128], P('row', 'col')
The draws below stay inside these ranges and needn't reach their ends.
Inputs may be any that keep to these rules, and one draw needn't show every extreme that they name: Chain c holds token slots c * 64 to (c + 1) * 64 - 1, of which the first chain_lengths[c] are present; the lengths sum to 384.
All inputs are finite; a program needn't handle non-finite values.
Results may differ from the reference program's by a relative error of at most 0.012.
Values may be sent and summed in bfloat16 or wider, within the bound.
A program may use at most 128 MiB of HBM per device.

```python
import math
import jax
import jax.numpy as jnp
import numpy as np
from jax import lax

C = 128
H = 4
DH = 32
HD = 128
N = 512
CHAINS = 8
SLOT = 64


def draw_att_bias(key, part):
    key = jax.random.fold_in(key, 7)
    base = jax.random.normal(key, (C, H), jnp.float32)
    return jnp.clip(base * (2.0 / math.sqrt(C)), -6.0, 6.0)


def shard_levels(stream_key, dims, cuts, smallest, top_value):
    def one(axis_at, parts):
        draws = jax.random.uniform(jax.random.fold_in(jax.random.fold_in(stream_key, 6), axis_at), (parts,), jnp.float32, smallest / len(cuts), top_value / len(cuts))
        return jnp.repeat(jnp.exp(draws), dims[axis_at] // parts).reshape((-1,) + (1,) * (len(dims) - axis_at - 1))

    gain = one(*cuts[0])
    for cut in cuts[1:]:
        gain = gain * one(*cut)
    return gain


def split_up(amount, total, limit, skew):
    portions = [(1 << 20) // math.isqrt(rank ** skew) + 1 for rank in range(2, amount + 1)]
    surplus, counts = total - limit - (amount - 1), [1] * (amount - 1)
    while surplus > 0:
        candidates = [i for i in range(amount - 1) if counts[i] < limit]
        mass, remaining = sum([portions[i] for i in candidates]), surplus
        for i in candidates:
            more = min(limit - counts[i], max(1, remaining * portions[i] // mass), surplus)
            counts[i] = counts[i] + more
            surplus = surplus - more
    return np.array([limit] + counts)


def ragged_sizes(rng, number_of, total, most, lean):
    if number_of == 2:
        one = jax.random.randint(rng, (), max(1, total - most), min(most, total - 1) + 1)
        return jnp.stack([one, total - one])
    sizes = jnp.asarray(split_up(number_of, total, most, lean), jnp.int32)
    couples = (number_of - 1) // 2
    source_of, sink = sizes[1:1 + 2 * couples:2], sizes[2:2 + 2 * couples:2]
    room = jnp.minimum(source_of - 1, most - sink)
    moved = jax.random.randint(jax.random.fold_in(rng, 1), (couples,), 0, 1 << 20) % (room + 1)
    sizes = sizes.at[1:1 + 2 * couples:2].set(source_of - moved).at[2:2 + 2 * couples:2].set(sink + moved)
    return sizes[jax.random.permutation(jax.random.fold_in(rng, 2), number_of)]


def normal_values(own_key, extent, scale, most, pieces=(), held_as=jnp.bfloat16):
    entries = scale * jax.random.normal(own_key, extent, jnp.float32)
    if pieces:
        entries = entries * shard_levels(own_key, extent, pieces, -0.22, 0.18)
    return jnp.clip(entries, -most, most).astype(held_as)


def setup_inputs(seed: int = 0) -> dict:
    arg_keys = jax.random.split(jax.random.key(seed), 8)
    return {
        "pair": normal_values(arg_keys[0], (N, N, C), 1.0, 6.0, ((0, 8), (1, 16)), jnp.float32),
        "chain_lengths": ragged_sizes(arg_keys[1], CHAINS, 3 * N // 4, SLOT, 2).astype(jnp.int32),
        "tri_in": normal_values(arg_keys[2], (C, 5 * C), C ** -0.5, 0.5),
        "tri_out": normal_values(arg_keys[3], (C, C), C ** -0.5, 0.5),
        "att_in": normal_values(arg_keys[4], (C, 4 * HD), C ** -0.5, 0.5),
        "att_bias": draw_att_bias(jax.random.fold_in(arg_keys[7], 71), 0),
        "att_out": normal_values(arg_keys[6], (HD, C), HD ** -0.5, 0.5),
    }


def layer_norm(values):
    center = values - lax.optimization_barrier(jnp.mean(values, axis=-1, keepdims=True))
    spread = lax.optimization_barrier(jnp.mean(center * center, axis=-1, keepdims=True))
    return center * lax.rsqrt(spread + 1e-05)

def token_present(chain_lengths, token_count):
    slot_size = token_count // CHAINS
    tokens = jnp.arange(token_count, dtype=jnp.int32)
    owner = (tokens // slot_size)[:, None] == jnp.arange(CHAINS, dtype=jnp.int32)[None, :]
    own_length = lax.optimization_barrier(jnp.sum(jnp.where(owner, chain_lengths[None, :], 0), axis=1))
    return (tokens % slot_size < own_length).astype(jnp.float32)

def reference(pair, chain_lengths, tri_in, tri_out, att_in, att_bias, att_out):
    token_count = pair.shape[0]
    width = pair.shape[2]
    present = token_present(chain_lengths, token_count)
    norm1 = layer_norm(pair).astype(jnp.bfloat16)
    proj = jnp.dot(norm1.reshape(-1, width), tri_in, preferred_element_type=jnp.float32)
    proj = proj.reshape(token_count, token_count, 5 * width)
    pair_mask = present[:, None, None] * present[None, :, None]
    left = (jax.nn.sigmoid(proj[..., :width]) * proj[..., width:2 * width] * pair_mask).astype(jnp.bfloat16)
    right = (jax.nn.sigmoid(proj[..., 2 * width:3 * width]) * proj[..., 3 * width:4 * width] * pair_mask).astype(jnp.bfloat16)
    out_gate = jax.nn.sigmoid(proj[..., 4 * width:])
    tri = jnp.einsum('ikc,jkc->ijc', left.astype(jnp.float32), right.astype(jnp.float32), precision=lax.Precision.HIGHEST)
    tri_norm = layer_norm(tri).astype(jnp.bfloat16)
    update = jnp.dot(tri_norm.reshape(-1, width), tri_out, preferred_element_type=jnp.float32)
    pair1 = pair + out_gate * update.reshape(token_count, token_count, width)
    norm2 = layer_norm(pair1).astype(jnp.bfloat16)
    qkvg = jnp.dot(norm2.reshape(-1, width), att_in, preferred_element_type=jnp.float32)
    qkvg = qkvg.reshape(token_count, token_count, 4 * HD)
    query = (qkvg[..., :HD] * DH ** (-0.5)).astype(jnp.bfloat16)
    keys = qkvg[..., HD:2 * HD].astype(jnp.bfloat16)
    values = qkvg[..., 2 * HD:3 * HD].astype(jnp.bfloat16)
    gate = jax.nn.sigmoid(qkvg[..., 3 * HD:])
    bias_flat = jnp.dot(norm2.reshape(-1, width).astype(jnp.float32), att_bias, precision=lax.Precision.HIGHEST)
    bias = jnp.transpose(bias_flat.reshape(token_count, token_count, H), (2, 0, 1))
    key_bias = (present - 1.0) * 1000000000.0

    def one_row(operands):
        query_row, key_row, value_row = operands
        query_heads = query_row.reshape(token_count, H, DH).astype(jnp.float32)
        key_heads = key_row.reshape(token_count, H, DH).astype(jnp.float32)
        value_heads = value_row.reshape(token_count, H, DH).astype(jnp.float32)
        score = jnp.einsum('jhd,khd->hjk', query_heads, key_heads, precision=lax.Precision.HIGHEST)
        score = score + bias + key_bias[None, None, :]
        top = lax.optimization_barrier(jnp.max(score, axis=-1, keepdims=True))
        expo = jnp.exp(score - top)
        denom = lax.optimization_barrier(jnp.sum(expo, axis=-1))
        rounded = lax.optimization_barrier(expo.astype(jnp.bfloat16)).astype(jnp.float32)
        summed = jnp.einsum('hjk,khd->hjd', rounded, value_heads, precision=lax.Precision.HIGHEST)
        result = summed / denom[..., None]
        return jnp.transpose(result, (1, 0, 2)).reshape(token_count, HD)
    attended = lax.map(one_row, (query, keys, values))
    gated = (gate * attended).astype(jnp.bfloat16)
    final = jnp.dot(gated.reshape(-1, HD), att_out, preferred_element_type=jnp.float32)
    return pair1 + final.reshape(token_count, token_count, width)
```

```python
import jax
import jax.numpy as jnp
from jax import lax
from jax.experimental import pallas as pl
from jax.experimental.pallas import tpu as pltpu
from jax.sharding import PartitionSpec as P

H = 4
DH = 32
CHAINS = 8
BF = jnp.bfloat16
F32 = jnp.float32


def token_present(chain_lengths, token_count):
    slot_size = token_count // CHAINS
    tokens = jnp.arange(token_count, dtype=jnp.int32)
    owner = (tokens // slot_size)[:, None] == jnp.arange(CHAINS, dtype=jnp.int32)[None, :]
    own_length = jnp.sum(jnp.where(owner, chain_lengths[None, :], 0), axis=1)
    return (tokens % slot_size < own_length).astype(jnp.float32)


def layer_norm(values, axis):
    center = values - jnp.mean(values, axis=axis, keepdims=True)
    spread = jnp.mean(center * center, axis=axis, keepdims=True)
    return center * lax.rsqrt(spread + 1e-05)


def nt(a, b):
    return lax.dot_general(a, b, (((1,), (1,)), ((), ())), preferred_element_type=F32)


def tn(a, b):
    return lax.dot_general(a, b, (((0,), (0,)), ((), ())), preferred_element_type=F32)


def nn(a, b):
    return lax.dot_general(a, b, (((1,), (0,)), ((), ())), preferred_element_type=F32)


def sigmoid(x):
    return 1.0 / (1.0 + jnp.exp(-x))


def lane_group(rows):
    return lax.broadcasted_iota(jnp.int32, (rows, 128), 1) // 32


def project_kernel(pair, weights, gate_weights, mask, send, gate, scratch):
    zero = jnp.zeros((64, 128), BF)
    for k in range(32):
        norm = layer_norm(pair[:, k, :], 1).astype(BF)
        twin = jnp.concatenate(
            [jnp.concatenate([norm, zero], 1), jnp.concatenate([zero, norm], 1)], 0
        )
        both = nt(weights[...], twin)
        out = sigmoid(both[:128]) * both[128:] * mask[k : k + 1, :]
        scratch[:, k, :] = out
        gate[:, k, :] = sigmoid(nn(norm, gate_weights[...]))
    for c in range(0, 128, 8):
        send[c : c + 8] = scratch[c : c + 8].astype(BF)


def product_kernel(got, send):
    group = lane_group(16)
    for r in range(8):
        left = got[r]
        for s in range(8):
            full = tn(left, got[s])[:64]
            parts = [full[g * 16 : (g + 1) * 16] for g in range(4)]
            for half in range(2):
                start = 64 + half * 32
                out = None
                for g in range(4):
                    shift = (g * 32 - start) % 128
                    piece = parts[g] if shift == 0 else pltpu.roll(parts[g], shift, 1)
                    out = piece if out is None else jnp.where(group == g, piece, out)
                send[r * 16 + s * 2 + half] = out.astype(BF)


def update_kernel(
    got, pair, gate, tri_out, packed_weights, bias_weights,
    pair1, send, bias, gate2, scratch,
):
    for c in range(0, 128, 8):
        scratch[c : c + 8] = got[c : c + 8].astype(F32)
    for g in range(4):
        cats = []
        for lo in range(g * 4, g * 4 + 4):
            normed = layer_norm(scratch[:, lo, :], 0).astype(BF)
            update = tn(normed, tri_out[...])
            blocks = []
            for hi in range(4):
                i = hi * 16 + lo
                new = pair[i] + gate[i] * update[hi * 32 : (hi + 1) * 32]
                pair1[i] = new
                blocks.append(layer_norm(new, 1).astype(BF))
            stacked = jnp.concatenate(blocks, 0)
            parts = nt(bias_weights[...], stacked)
            for h in range(H):
                bias[h, lo : lo + 1, :] = (
                    parts[h : h + 1] + (parts[8 + h : 9 + h] + parts[16 + h : 17 + h])
                )
            cats.append(jnp.concatenate(blocks, 1))
        rows = jnp.concatenate(cats, 0)
        for t in range(4):
            for h in range(H):
                at = (t * 4 + h) * 128
                out = nn(rows, packed_weights[:, at : at + 128])
                if t == 0:
                    out = out * (DH ** (-0.5))
                if t == 3:
                    gate2[g, h] = sigmoid(out)
                else:
                    send[h * 4 + g, t] = out.astype(BF)


def bias_kernel(got, key_bias, out):
    group = lane_group(16)
    for quad in range(4):
        for hi in range(4):
            row = None
            for q in range(4):
                piece = got[quad * 4 + q]
                shift = (q * 32 - hi * 32) % 128
                piece = piece if shift == 0 else pltpu.roll(piece, shift, 1)
                row = piece if row is None else jnp.where(group == q, piece, row)
            lanes = slice(quad * 128, quad * 128 + 128)
            out[hi * 16 : hi * 16 + 16, lanes] = row + key_bias[:, lanes]


BLOCK = 128


def attend_kernel(got, bias, out):
    group = lane_group(BLOCK)
    span = BLOCK // 32
    ones = jnp.ones((512, 128), BF)

    def row(i4, _):
        at = pl.ds(pl.multiple_of(i4 * 32, 32), 32)
        keys = got[:, 1, at, :].reshape(512, 128)
        values = jnp.concatenate([got[:, 2, at, :].reshape(512, 128), ones], 1)
        for block in range(512 // BLOCK):
            query = got[block * span : (block + 1) * span, 0, at, :].reshape(BLOCK, 128)
            total = None
            for g in range(4):
                mine = jnp.where(group == g, query, jnp.zeros_like(query))
                score = nt(mine, keys) + bias[block * BLOCK : (block + 1) * BLOCK, :]
                top = jnp.max(score, axis=1, keepdims=True)
                weights = jnp.exp(score - top).astype(BF)
                summed = nn(weights, values)
                result = summed[:, :128] / summed[:, 128:]
                total = result if total is None else jnp.where(group == g, result, total)
            out[block * span : (block + 1) * span, at, :] = total.astype(BF).reshape(span, 32, 128)
        return 0

    lax.fori_loop(0, 4, row, 0)


def finish_kernel(got, gate2, pair1, out_weights, out):
    for g in range(4):
        gated = jnp.concatenate(
            [(gate2[g, h] * got[h * 4 + g].astype(F32)).astype(BF) for h in range(H)], 1
        )
        result = nn(gated, out_weights[...])
        for hi in range(4):
            at = slice(hi * 16 + g * 4, hi * 16 + g * 4 + 4)
            out[at] = pair1[at] + result[:, hi * 128 : (hi + 1) * 128].reshape(4, 32, 128)


def call(kernel, outs, *args, scratch=(), name):
    vmem = pl.BlockSpec(memory_space=pltpu.VMEM)
    single = not isinstance(outs, tuple)
    return pl.pallas_call(
        kernel,
        out_shape=outs,
        in_specs=[vmem] * len(args),
        out_specs=vmem if single else (vmem,) * len(outs),
        scratch_shapes=scratch,
        name=name,
        compiler_params=pltpu.CompilerParams(vmem_limit_bytes=48 << 20),
    )(*args)


def shape(*dims, dtype=BF):
    return jax.ShapeDtypeStruct(dims, dtype)


def on_device(pair, chain_lengths, tri_in, tri_out, att_in, att_bias, att_out):
    row_start = lax.axis_index("row") * 64
    col_start = lax.axis_index("col") * 32
    present = token_present(chain_lengths, 512)
    row_present = lax.dynamic_slice_in_dim(present, row_start, 64)
    col_present = lax.dynamic_slice_in_dim(present, col_start, 32)
    mask = col_present[:, None] * jnp.concatenate([row_present, row_present])[None, :]
    key_bias = ((present - 1.0) * 1000000000.0)[None, :]

    pg, pv, qg, qv, og = (tri_in[:, n * 128 : (n + 1) * 128] for n in range(5))
    weights = jnp.concatenate(
        [jnp.concatenate([pg.T, qg.T], 1), jnp.concatenate([pv.T, qv.T], 1)], 0
    )
    eye = jnp.eye(4, dtype=BF)
    packed = att_in.reshape(1, 128, 4, H, 1, DH) * eye.reshape(4, 1, 1, 1, 4, 1)
    packed = packed.reshape(512, 2048)
    out_weights = att_out.reshape(H, 1, DH, 1, 128) * eye.reshape(1, 4, 1, 4, 1)
    out_weights = out_weights.reshape(512, 512)
    high = lax.reduce_precision(att_bias, 8, 7)
    rest = att_bias - high
    middle = lax.reduce_precision(rest, 8, 7)
    low = rest - middle
    pad = jnp.zeros((4, 128), BF)
    bias_weights = jnp.concatenate(
        [high.T.astype(BF), pad, middle.T.astype(BF), pad, low.T.astype(BF), pad], 0
    )

    send, gate = call(
        project_kernel,
        (shape(128, 32, 128), shape(64, 32, 128, dtype=F32)),
        pair, weights, og, mask,
        scratch=[pltpu.VMEM((128, 32, 128), F32)],
        name="project",
    )
    got = lax.all_to_all(send, ("row", "col"), 0, 0, tiled=True)
    send = call(product_kernel, shape(128, 16, 128), got.reshape(8, 512, 128), name="product")
    got = lax.all_to_all(send, ("row", "col"), 0, 0, tiled=True)
    pair1, send, bias, gate2 = call(
        update_kernel,
        (
            shape(64, 32, 128, dtype=F32),
            shape(16, 3, 128, 128),
            shape(4, 16, 128, dtype=F32),
            shape(4, 4, 128, 128, dtype=F32),
        ),
        got, pair, gate, tri_out, packed, bias_weights,
        scratch=[pltpu.VMEM((128, 16, 128), F32)],
        name="update",
    )
    bias_send = jnp.broadcast_to(bias[:, None], (4, 4, 16, 128)).reshape(16, 16, 128)
    bias_got = lax.all_to_all(bias_send, "col", 0, 0, tiled=True)
    bias_rows = call(bias_kernel, shape(64, 512, dtype=F32), bias_got, key_bias, name="bias")
    bias_send = jnp.broadcast_to(bias_rows[None], (8, 64, 512))
    bias_all = lax.all_to_all(bias_send, "row", 0, 0, tiled=True)
    got = lax.all_to_all(send, "col", 0, 0, tiled=True)
    send = call(
        attend_kernel, shape(16, 128, 128), got, bias_all.reshape(512, 512), name="attend"
    )
    got = lax.all_to_all(send, "col", 0, 0, tiled=True)
    return call(
        finish_kernel,
        shape(64, 32, 128, dtype=F32),
        got, gate2, pair1, out_weights,
        name="finish",
    )


def solution(mesh):
    return jax.shard_map(
        on_device,
        mesh=mesh,
        in_specs=(P("row", "col", None), P(), P(), P(), P(), P(), P()),
        out_specs=P("row", "col", None),
        check_vma=False,
    )
```

```python
import jax
import jax.numpy as jnp
from jax import lax
from jax.experimental import pallas as pl
from jax.experimental.pallas import tpu as pltpu
from jax.sharding import PartitionSpec as P

MESH = pl.DeviceIdType.MESH
H = 4
DH = 32
ROWS = 8
COLS = 16
BF = jnp.bfloat16
F32 = jnp.float32
BLOCK = 128
TRI, BACK, QKV, BIAS_COL, BIAS_ROW, HEADS = range(6)


def layer_norm(values, axis):
    center = values - jnp.mean(values, axis=axis, keepdims=True)
    spread = jnp.mean(center * center, axis=axis, keepdims=True)
    return center * lax.rsqrt(spread + 1e-05)


def nt(a, b):
    return lax.dot_general(a, b, (((1,), (1,)), ((), ())), preferred_element_type=F32)


def tn(a, b):
    return lax.dot_general(a, b, (((0,), (0,)), ((), ())), preferred_element_type=F32)


def nn(a, b):
    return lax.dot_general(a, b, (((1,), (0,)), ((), ())), preferred_element_type=F32)


def sigmoid(x):
    return 1.0 / (1.0 + jnp.exp(-x))


def lane_group(rows):
    return lax.broadcasted_iota(jnp.int32, (rows, 128), 1) // 32


def roll(x, shift):
    return x if shift % 128 == 0 else pltpu.roll(x, shift % 128, 1)


def block_kernel(
    pair, lengths, tri_in, tri_out, att_in, att_bias, att_out, out,
    tri_send, tri_got, back_send, back_got, qkv_send, qkv_got,
    bias_send, bias_got, bias_rows, bias_all, head_send, head_got,
    wide, gate, gate2, pair1, normed2, packed, out_packed, send_sem, recv_sem,
):
    row, col = lax.axis_index("row"), lax.axis_index("col")
    me = row * COLS + col

    def anyone(t):
        return lax.rem(row + t // COLS, ROWS), lax.rem(col + lax.rem(t, COLS), COLS)

    def each(start, stop, body):
        def step(t, carry):
            body(t)
            return carry

        lax.fori_loop(start, stop, step, 0)

    def push(phase, src, dst, device):
        pltpu.make_async_remote_copy(
            src_ref=src, dst_ref=dst, send_sem=send_sem.at[phase], recv_sem=recv_sem.at[phase],
            device_id=device, device_id_type=MESH,
        ).start()

    def landed(phase, ref):
        pltpu.make_async_copy(ref, ref, recv_sem.at[phase]).wait()

    def sent(phase, ref):
        pltpu.make_async_copy(ref, ref, send_sem.at[phase]).wait()

    barrier = pltpu.get_barrier_semaphore()

    def greet(t):
        pl.semaphore_signal(barrier, inc=1, device_id=anyone(t), device_id_type=MESH)

    each(1, ROWS * COLS, greet)

    columns = [tri_in[:, n * 128 : (n + 1) * 128] for n in range(5)]
    turned = [jnp.transpose(block.astype(F32)).astype(BF) for block in columns[:4]]
    weights = jnp.concatenate(
        [
            jnp.concatenate([turned[0], turned[2]], 1),
            jnp.concatenate([turned[1], turned[3]], 1),
        ],
        0,
    )
    lane = lax.broadcasted_iota(jnp.int32, (1, 128), 1)
    row_present = (lax.rem(lane, 64) < lengths[row]).astype(F32)
    col_length = lengths[col // 2] - lax.rem(col, 2) * 32
    zero = jnp.zeros((64, 128), BF)
    for k in range(32):
        norm = layer_norm(pair[:, k, :], 1).astype(BF)
        twin = jnp.concatenate(
            [jnp.concatenate([norm, zero], 1), jnp.concatenate([zero, norm], 1)], 0
        )
        both = nt(weights, twin)
        mask = row_present * jnp.where(k < col_length, 1.0, 0.0)
        wide[:, k, :] = sigmoid(both[:128]) * both[128:] * mask
    for c in range(0, 128, 16):
        tri_send[c : c + 16] = wide[c : c + 16].astype(BF)

    pl.semaphore_wait(barrier, ROWS * COLS - 1)

    def push_tri(t):
        r, c = anyone(t)
        push(TRI, tri_send.at[r * COLS + c], tri_got.at[me], (r, c))

    each(1, ROWS * COLS, push_tri)
    tri_got[me] = tri_send[me]

    for k in range(32):
        norm = layer_norm(pair[:, k, :], 1).astype(BF)
        gate[:, k, :] = sigmoid(nn(norm, columns[4]))
    group = lane_group(128)
    for t in range(4):
        block = att_in[:, t * 128 : (t + 1) * 128].astype(F32)
        for distance in range(4):
            moved = roll(block, distance * 32)
            for h in range(H):
                g = (h + distance) % 4
                at = (t * 4 + h) * 128
                packed[g * 128 : (g + 1) * 128, at : at + 128] = jnp.where(
                    group == g, moved, 0.0
                ).astype(BF)
    out_packed[...] = jnp.zeros_like(out_packed)
    for h in range(H):
        for g in range(4):
            at = h * 128 + g * 32
            out_packed[at : at + 32, g * 128 : (g + 1) * 128] = att_out[h * 32 : (h + 1) * 32, :]
    rest = att_bias[...]
    bias_weights = []
    for _ in range(3):
        part = rest.astype(BF)
        rest = rest - part.astype(F32)
        bias_weights.append(part)

    landed(TRI, tri_got.at[pl.ds(0, ROWS * COLS - 1)])
    group = lane_group(16)

    def product(r):
        left = tri_got[pl.ds(r * COLS, COLS)].reshape(512, 128)
        for s in range(ROWS):
            full = tn(left, tri_got[s * COLS : (s + 1) * COLS].reshape(512, 128))
            parts = [full[g * 16 : (g + 1) * 16] for g in range(4)]
            for half in range(2):
                packed_rows = None
                for g in range(4):
                    piece = roll(parts[g], g * 32 - 64 - half * 32)
                    packed_rows = piece if g == 0 else jnp.where(group == g, piece, packed_rows)
                back_send[r * COLS + s * 2 + half] = packed_rows.astype(BF)

    each(0, ROWS, product)

    def push_back(t):
        r, c = anyone(t)
        push(BACK, back_send.at[r * COLS + c], back_got.at[me], (r, c))

    each(1, ROWS * COLS, push_back)
    back_got[me] = back_send[me]
    landed(BACK, back_got.at[pl.ds(0, ROWS * COLS - 1)])

    for c in range(0, 128, 16):
        wide[c : c + 16, 0:16] = back_got[c : c + 16].astype(F32)
    for g in range(4):
        cats = []
        for lo in range(g * 4, g * 4 + 4):
            update = tn(layer_norm(wide[:, lo, :], 0).astype(BF), tri_out[...])
            blocks = []
            for hi in range(4):
                i = hi * 16 + lo
                new = pair[i] + gate[i] * update[hi * 32 : (hi + 1) * 32]
                pair1[i] = new
                blocks.append(layer_norm(new, 1).astype(BF))
            stacked = jnp.concatenate(blocks, 0)
            parts = [nt(w, stacked) for w in bias_weights]
            bias = parts[0] + (parts[1] + parts[2])
            for h in range(H):
                bias_send[h, lo : lo + 1, :] = bias[h : h + 1]
            cats.append(jnp.concatenate(blocks, 1))
        normed2[g] = jnp.concatenate(cats, 0)

    def push_bias_col(t):
        c = lax.rem(col + t, COLS)
        push(BIAS_COL, bias_send.at[c // 4], bias_got.at[col], (row, c))

    each(1, COLS, push_bias_col)
    bias_got[col] = bias_send[col // 4]

    for g in range(4):
        for t in range(3):
            for h in range(H):
                at = (t * 4 + h) * 128
                block = nn(normed2[g], packed[:, at : at + 128])
                if t == 0:
                    block = block * (DH ** (-0.5))
                qkv_send[h * 4 + g, t] = block.astype(BF)

    def push_qkv(t):
        c = lax.rem(col + t, COLS)
        push(QKV, qkv_send.at[c], qkv_got.at[col], (row, c))

    each(1, COLS, push_qkv)

    landed(BIAS_COL, bias_got.at[pl.ds(0, COLS - 1)])
    for quad in range(4):
        lanes = slice(quad * 128, quad * 128 + 128)
        length = jnp.where(lane < 64, lengths[quad * 2], lengths[quad * 2 + 1])
        key_bias = jnp.where(lax.rem(lane, 64) < length, 0.0, -1000000000.0)
        for hi in range(4):
            rows = None
            for q in range(4):
                piece = roll(bias_got[quad * 4 + q], q * 32 - hi * 32)
                rows = piece if q == 0 else jnp.where(group == q, piece, rows)
            bias_rows[hi * 16 : hi * 16 + 16, lanes] = rows + key_bias

    def push_bias_row(t):
        r = lax.rem(row + t, ROWS)
        push(BIAS_ROW, bias_rows, bias_all.at[row], (r, col))

    each(1, ROWS, push_bias_row)
    bias_all[row] = bias_rows[...]
    qkv_got[col] = qkv_send[col]

    for g in range(4):
        for h in range(H):
            at = (12 + h) * 128
            gate2[g, h] = sigmoid(nn(normed2[g], packed[:, at : at + 128]))

    landed(QKV, qkv_got.at[pl.ds(0, COLS - 1)])
    landed(BIAS_ROW, bias_all.at[pl.ds(0, ROWS - 1)])

    group = lane_group(BLOCK)
    span = BLOCK // 32
    ones = jnp.ones((512, 128), BF)

    def attend(i4):
        at = pl.ds(pl.multiple_of(i4 * 32, 32), 32)
        keys = qkv_got[:, 1, at, :].reshape(512, 128)
        values = jnp.concatenate([qkv_got[:, 2, at, :].reshape(512, 128), ones], 1)
        for block in range(512 // BLOCK):
            chunk = slice(block * span, (block + 1) * span)
            query = qkv_got[chunk, 0, at, :].reshape(BLOCK, 128)
            bias = bias_all[block * BLOCK // 64 : (block + 1) * BLOCK // 64].reshape(BLOCK, 512)
            total = None
            for g in range(4):
                mine = jnp.where(group == g, query, jnp.zeros_like(query))
                score = nt(mine, keys) + bias
                top = jnp.max(score, axis=1, keepdims=True)
                summed = nn(jnp.exp(score - top).astype(BF), values)
                result = summed[:, :128] / summed[:, 128:]
                total = result if g == 0 else jnp.where(group == g, result, total)
            head_send[chunk, at, :] = total.astype(BF).reshape(span, 32, 128)

        def push_heads(t):
            c = lax.rem(col + t, COLS)
            push(HEADS, head_send.at[c, at], head_got.at[col, at], (row, c))

        each(1, COLS, push_heads)

    each(0, 4, attend)
    head_got[col] = head_send[col]
    landed(HEADS, head_got.at[pl.ds(0, COLS - 1)])

    for g in range(4):
        gated = jnp.concatenate(
            [(gate2[g, h] * head_got[h * 4 + g].astype(F32)).astype(BF) for h in range(H)], 1
        )
        result = nn(gated, out_packed[...])
        for hi in range(4):
            rows = slice(hi * 16 + g * 4, hi * 16 + g * 4 + 4)
            out[rows] = pair1[rows] + result[:, hi * 128 : (hi + 1) * 128].reshape(4, 32, 128)

    sent(TRI, tri_send.at[pl.ds(0, ROWS * COLS - 1)])
    sent(BACK, back_send.at[pl.ds(0, ROWS * COLS - 1)])
    sent(QKV, qkv_send.at[pl.ds(0, COLS - 1)])
    sent(BIAS_COL, bias_got.at[pl.ds(0, COLS - 1)])
    sent(BIAS_ROW, bias_all.at[pl.ds(0, ROWS - 1)])
    sent(HEADS, head_send.at[pl.ds(0, COLS - 1)])


def on_device(pair, chain_lengths, tri_in, tri_out, att_in, att_bias, att_out):
    vmem = pl.BlockSpec(memory_space=pltpu.VMEM)
    return pl.pallas_call(
        block_kernel,
        out_shape=jax.ShapeDtypeStruct((64, 32, 128), F32),
        in_specs=[vmem, pl.BlockSpec(memory_space=pltpu.SMEM)] + [vmem] * 5,
        out_specs=vmem,
        scratch_shapes=[
            pltpu.VMEM((128, 32, 128), BF),
            pltpu.VMEM((128, 32, 128), BF),
            pltpu.VMEM((128, 16, 128), BF),
            pltpu.VMEM((128, 16, 128), BF),
            pltpu.VMEM((16, 3, 128, 128), BF),
            pltpu.VMEM((16, 3, 128, 128), BF),
            pltpu.VMEM((4, 16, 128), F32),
            pltpu.VMEM((16, 16, 128), F32),
            pltpu.VMEM((64, 512), F32),
            pltpu.VMEM((8, 64, 512), F32),
            pltpu.VMEM((16, 128, 128), BF),
            pltpu.VMEM((16, 128, 128), BF),
            pltpu.VMEM((128, 32, 128), F32),
            pltpu.VMEM((64, 32, 128), F32),
            pltpu.VMEM((4, 4, 128, 128), F32),
            pltpu.VMEM((64, 32, 128), F32),
            pltpu.VMEM((4, 128, 512), BF),
            pltpu.VMEM((512, 2048), BF),
            pltpu.VMEM((512, 512), BF),
            pltpu.SemaphoreType.DMA((6,)),
            pltpu.SemaphoreType.DMA((6,)),
        ],
        name="pairformer",
        compiler_params=pltpu.CompilerParams(
            collective_id=0, has_side_effects=True, vmem_limit_bytes=48 << 20
        ),
    )(pair, chain_lengths, tri_in, tri_out, att_in, att_bias.T, att_out)


def solution(mesh):
    return jax.shard_map(
        on_device,
        mesh=mesh,
        in_specs=(P("row", "col", None), P(), P(), P(), P(), P(), P()),
        out_specs=P("row", "col", None),
        check_vma=False,
    )
```

```python
import jax
import jax.numpy as jnp
from jax import lax
from jax.experimental import pallas as pl
from jax.experimental.pallas import tpu as pltpu
from jax.sharding import PartitionSpec as P

MESH = pl.DeviceIdType.MESH
H = 4
DH = 32
ROWS = 8
COLS = 16
BF = jnp.bfloat16
F32 = jnp.float32
BLOCK = 128
TRI, BACK, NORM, BIAS_COL, BIAS_ROW, BIAS_TWIN, HEADS = range(7)


def layer_norm(values, axis):
    center = values - jnp.mean(values, axis=axis, keepdims=True)
    spread = jnp.mean(center * center, axis=axis, keepdims=True)
    return center * lax.rsqrt(spread + 1e-05)


def nt(a, b):
    return lax.dot_general(a, b, (((1,), (1,)), ((), ())), preferred_element_type=F32)


def tn(a, b):
    return lax.dot_general(a, b, (((0,), (0,)), ((), ())), preferred_element_type=F32)


def nn(a, b):
    return lax.dot_general(a, b, (((1,), (0,)), ((), ())), preferred_element_type=F32)


def sigmoid(x):
    return 1.0 / (1.0 + jnp.exp(-x))


def lane_group(rows):
    return lax.broadcasted_iota(jnp.int32, (rows, 128), 1) // 32


def roll(x, shift):
    return x if shift % 128 == 0 else pltpu.roll(x, shift % 128, 1)


def block_kernel(
    lengths, pair_in, tri_in_in, tri_out_in, att_in_in, att_bias_in, att_out_in, out,
    pair, tri_in, tri_out, att_in, att_bias, att_out,
    tri_send, tri_got, back_send, back_got, norm_send, norm_got,
    bias_send, bias_got, bias_rows, bias_all, head_send, head_got,
    wide, gate, gate2, pair1, packed, gate_packed, out_packed, load_sem, send_sem, recv_sem,
):
    row, col = lax.axis_index("row"), lax.axis_index("col")
    me = row * COLS + col

    loads = [
        pltpu.make_async_copy(src, dst, load_sem.at[n])
        for n, (src, dst) in enumerate(
            [
                (pair_in, pair), (tri_in_in, tri_in), (att_in_in, att_in),
                (att_out_in, att_out), (att_bias_in, att_bias), (tri_out_in, tri_out),
            ]
        )
    ]
    for load in loads:
        load.start()

    def anyone(t):
        return lax.rem(row + t // COLS, ROWS), lax.rem(col + lax.rem(t, COLS), COLS)

    def each(start, stop, body):
        def step(t, carry):
            body(t)
            return carry

        lax.fori_loop(start, stop, step, 0)

    def push(phase, src, dst, device):
        pltpu.make_async_remote_copy(
            src_ref=src, dst_ref=dst, send_sem=send_sem.at[phase], recv_sem=recv_sem.at[phase],
            device_id=device, device_id_type=MESH,
        ).start()

    def landed(phase, ref):
        pltpu.make_async_copy(ref, ref, recv_sem.at[phase]).wait()

    def sent(phase, ref):
        pltpu.make_async_copy(ref, ref, send_sem.at[phase]).wait()

    barrier = pltpu.get_barrier_semaphore()

    def greet(t):
        pl.semaphore_signal(barrier, inc=1, device_id=anyone(t), device_id_type=MESH)

    each(1, ROWS * COLS, greet)

    loads[1].wait()
    columns = [tri_in[:, n * 128 : (n + 1) * 128] for n in range(5)]
    turned = [jnp.transpose(block.astype(F32)).astype(BF) for block in columns[:4]]
    weights = jnp.concatenate(
        [
            jnp.concatenate([turned[0], turned[2]], 1),
            jnp.concatenate([turned[1], turned[3]], 1),
        ],
        0,
    )
    lane = lax.broadcasted_iota(jnp.int32, (1, 128), 1)
    row_present = (lax.rem(lane, 64) < lengths[row]).astype(F32)
    col_length = lengths[col // 2] - lax.rem(col, 2) * 32
    zero = jnp.zeros((64, 128), BF)
    loads[0].wait()
    for k in range(32):
        norm = layer_norm(pair[:, k, :], 1).astype(BF)
        twin = jnp.concatenate(
            [jnp.concatenate([norm, zero], 1), jnp.concatenate([zero, norm], 1)], 0
        )
        both = nt(weights, twin)
        mask = row_present * jnp.where(k < col_length, 1.0, 0.0)
        wide[:, k, :] = sigmoid(both[:128]) * both[128:] * mask
    for c in range(0, 128, 16):
        tri_send[c : c + 16] = wide[c : c + 16].astype(BF)

    pl.semaphore_wait(barrier, ROWS * COLS - 1)

    def push_tri(t):
        r, c = anyone(t)
        push(TRI, tri_send.at[r * COLS + c], tri_got.at[me], (r, c))

    each(1, ROWS * COLS, push_tri)
    tri_got[me] = tri_send[me]

    for k in range(32):
        norm = layer_norm(pair[:, k, :], 1).astype(BF)
        gate[:, k, :] = sigmoid(nn(norm, columns[4]))
    for load in loads[2:]:
        load.wait()
    group = lane_group(128)
    mine_first = jnp.where(col // 8 == 0, 1.0, 0.0)
    for t in range(4):
        block = att_in[:, t * 128 : (t + 1) * 128].astype(F32)
        low = jnp.where(group < 2, block, 0.0)
        high = jnp.where(group < 2, 0.0, block)
        low_up, high_down = roll(low, 64), roll(high, 64)
        if t == 3:
            gate_packed[0:128, 0:128] = low.astype(BF)
            gate_packed[128:256, 0:128] = low_up.astype(BF)
            gate_packed[0:128, 128:256] = high_down.astype(BF)
            gate_packed[128:256, 128:256] = high.astype(BF)
        else:
            at = slice(t * 128, t * 128 + 128)
            packed[0:128, at] = jnp.where(mine_first > 0.5, low, high_down).astype(BF)
            packed[128:256, at] = jnp.where(mine_first > 0.5, low_up, high).astype(BF)
    out_packed[...] = jnp.zeros_like(out_packed)
    for p in range(2):
        for i in range(2):
            at = p * 128 + i * 64
            out_packed[at : at + 64, i * 128 : (i + 1) * 128] = att_out[p * 64 : p * 64 + 64, :]
    rest = att_bias[...]
    bias_weights = []
    for _ in range(3):
        part = rest.astype(BF)
        rest = rest - part.astype(F32)
        bias_weights.append(part)

    landed(TRI, tri_got.at[pl.ds(0, ROWS * COLS - 1)])
    group = lane_group(16)

    def product(r):
        left = tri_got[pl.ds(r * COLS, COLS)].reshape(512, 128)
        for s in range(ROWS):
            full = tn(left, tri_got[s * COLS : (s + 1) * COLS].reshape(512, 128))
            parts = [full[g * 16 : (g + 1) * 16] for g in range(4)]
            for half in range(2):
                packed_rows = None
                for g in range(4):
                    piece = roll(parts[g], g * 32 - 64 - half * 32)
                    packed_rows = piece if g == 0 else jnp.where(group == g, piece, packed_rows)
                back_send[r * COLS + s * 2 + half] = packed_rows.astype(BF)

    each(0, ROWS, product)

    def push_back(t):
        r, c = anyone(t)
        push(BACK, back_send.at[r * COLS + c], back_got.at[me], (r, c))

    each(1, ROWS * COLS, push_back)
    back_got[me] = back_send[me]
    landed(BACK, back_got.at[pl.ds(0, ROWS * COLS - 1)])

    for c in range(0, 128, 16):
        wide[c : c + 16, 0:16] = back_got[c : c + 16].astype(F32)
    for lo in range(16):
        update = tn(layer_norm(wide[:, lo, :], 0).astype(BF), tri_out[...])
        blocks = []
        for hi in range(4):
            i = hi * 16 + lo
            new = pair[i] + gate[i] * update[hi * 32 : (hi + 1) * 32]
            pair1[i] = new
            block = layer_norm(new, 1).astype(BF)
            at = (lo % 2) * 64 + (hi // 2) * 32
            norm_send[lo // 2, at : at + 32, (hi % 2) * 128 : (hi % 2) * 128 + 128] = block
            blocks.append(block)
        stacked = jnp.concatenate(blocks, 0)
        parts = [nt(w, stacked) for w in bias_weights]
        bias = parts[0] + (parts[1] + parts[2])
        for h in range(H):
            bias_send[h, lo : lo + 1, :] = bias[h : h + 1]

    def push_bias_col(t):
        c = lax.rem(col + t, COLS)
        push(BIAS_COL, bias_send.at[c // 8 * 2 + lax.rem(c, 2)], bias_got.at[col], (row, c))

    each(1, COLS, push_bias_col)
    head = lax.rem(col, 2)
    bias_got[col] = bias_send[col // 8 * 2 + head]

    def push_norm(t):
        c = lax.rem(col + t, COLS)
        push(NORM, norm_send.at[lax.rem(c, 8)], norm_got.at[col], (row, c))

    each(1, COLS, push_norm)

    landed(BIAS_COL, bias_got.at[pl.ds(0, COLS - 1)])
    for quad in range(4):
        lanes = slice(quad * 128, quad * 128 + 128)
        length = jnp.where(lane < 64, lengths[quad * 2], lengths[quad * 2 + 1])
        key_bias = jnp.where(lax.rem(lane, 64) < length, 0.0, -1000000000.0)
        for hi in range(4):
            rows = None
            for q in range(4):
                piece = roll(bias_got[quad * 4 + q], q * 32 - hi * 32)
                rows = piece if q == 0 else jnp.where(group == q, piece, rows)
            bias_rows[hi * 16 : hi * 16 + 16, lanes] = rows + key_bias

    def push_bias_row(t):
        r = lax.rem(row + t, ROWS)
        push(BIAS_ROW, bias_rows, bias_all.at[head, row], (r, col))

    each(1, ROWS, push_bias_row)
    bias_all[head, row] = bias_rows[...]
    norm_got[col] = norm_send[lax.rem(col, 8)]

    for g in range(8):
        gate2[g] = sigmoid(nn(norm_send[g], gate_packed[...]))

    landed(BIAS_ROW, bias_all.at[0, pl.ds(0, ROWS - 1)])
    push(BIAS_TWIN, bias_all.at[head], bias_all.at[head], (row, col + 1 - 2 * head))
    landed(NORM, norm_got.at[pl.ds(0, COLS - 1)])
    landed(BIAS_TWIN, bias_all.at[0])
    group = lane_group(BLOCK)
    span = BLOCK // 32
    ones = jnp.ones((512, 128), BF)

    def attend(i4):
        at = pl.ds(pl.multiple_of(i4 * 32, 32), 32)
        normed = norm_got[:, at, :].reshape(512, 256)
        queries = (nn(normed, packed[:, 0:128]) * (DH ** (-0.5))).astype(BF)
        keys = nn(normed, packed[:, 128:256]).astype(BF)
        values = jnp.concatenate([nn(normed, packed[:, 256:384]).astype(BF), ones], 1)
        for block in range(512 // BLOCK):
            chunk = slice(block * span, (block + 1) * span)
            query = queries[block * BLOCK : (block + 1) * BLOCK]
            rows = slice(block * BLOCK // 64, (block + 1) * BLOCK // 64)
            total = None
            for g in range(4):
                mine = jnp.where(group == g, query, jnp.zeros_like(query))
                score = nt(mine, keys) + bias_all[g % 2, rows].reshape(BLOCK, 512)
                top = jnp.max(score, axis=1, keepdims=True)
                summed = nn(jnp.exp(score - top).astype(BF), values)
                result = summed[:, :128] / summed[:, 128:]
                total = result if g == 0 else jnp.where(group == g, result, total)
            head_send[chunk, at, :] = total.astype(BF).reshape(span, 32, 128)

        def push_heads(t):
            c = lax.rem(col + t, COLS)
            push(HEADS, head_send.at[c, at], head_got.at[col, at], (row, c))

        each(1, COLS, push_heads)

    each(0, 4, attend)
    head_got[col] = head_send[col]
    landed(HEADS, head_got.at[pl.ds(0, COLS - 1)])

    for g in range(8):
        heads = jnp.concatenate([head_got[g], head_got[8 + g]], 1).astype(F32)
        result = nn((gate2[g] * heads).astype(BF), out_packed[...])
        for l in range(2):
            for hi in range(4):
                i = hi * 16 + g * 2 + l
                at = l * 64 + (hi // 2) * 32
                lanes = slice((hi % 2) * 128, (hi % 2) * 128 + 128)
                out[i] = pair1[i] + result[at : at + 32, lanes]

    sent(TRI, tri_send.at[pl.ds(0, ROWS * COLS - 1)])
    sent(BACK, back_send.at[pl.ds(0, ROWS * COLS - 1)])
    sent(NORM, norm_got.at[pl.ds(0, COLS - 1)])
    sent(BIAS_COL, bias_got.at[pl.ds(0, COLS - 1)])
    sent(BIAS_ROW, bias_all.at[0, pl.ds(0, ROWS - 1)])
    sent(BIAS_TWIN, bias_all.at[0])
    sent(HEADS, head_send.at[pl.ds(0, COLS - 1)])


def on_device(pair, chain_lengths, tri_in, tri_out, att_in, att_bias, att_out):
    vmem = pl.BlockSpec(memory_space=pltpu.VMEM)
    return pl.pallas_call(
        block_kernel,
        out_shape=jax.ShapeDtypeStruct((64, 32, 128), F32),
        in_specs=[pl.BlockSpec(memory_space=pltpu.SMEM)] + [pl.BlockSpec(memory_space=pltpu.HBM)] * 6,
        out_specs=vmem,
        scratch_shapes=[
            pltpu.VMEM((64, 32, 128), F32),
            pltpu.VMEM((128, 640), BF),
            pltpu.VMEM((128, 128), BF),
            pltpu.VMEM((128, 512), BF),
            pltpu.VMEM((4, 128), F32),
            pltpu.VMEM((128, 128), BF),
            pltpu.VMEM((128, 32, 128), BF),
            pltpu.VMEM((128, 32, 128), BF),
            pltpu.VMEM((128, 16, 128), BF),
            pltpu.VMEM((128, 16, 128), BF),
            pltpu.VMEM((8, 128, 256), BF),
            pltpu.VMEM((16, 128, 256), BF),
            pltpu.VMEM((4, 16, 128), F32),
            pltpu.VMEM((16, 16, 128), F32),
            pltpu.VMEM((64, 512), F32),
            pltpu.VMEM((2, 8, 64, 512), F32),
            pltpu.VMEM((16, 128, 128), BF),
            pltpu.VMEM((16, 128, 128), BF),
            pltpu.VMEM((128, 32, 128), F32),
            pltpu.VMEM((64, 32, 128), F32),
            pltpu.VMEM((8, 128, 256), F32),
            pltpu.VMEM((64, 32, 128), F32),
            pltpu.VMEM((256, 384), BF),
            pltpu.VMEM((256, 256), BF),
            pltpu.VMEM((256, 256), BF),
            pltpu.SemaphoreType.DMA((6,)),
            pltpu.SemaphoreType.DMA((7,)),
            pltpu.SemaphoreType.DMA((7,)),
        ],
        name="pairformer",
        compiler_params=pltpu.CompilerParams(
            collective_id=0, has_side_effects=True, vmem_limit_bytes=63 << 20
        ),
    )(chain_lengths, pair, tri_in, tri_out, att_in, att_bias.T, att_out)


def solution(mesh):
    return jax.shard_map(
        on_device,
        mesh=mesh,
        in_specs=(P("row", "col", None), P(), P(), P(), P(), P(), P()),
        out_specs=P("row", "col", None),
        check_vma=False,
    )
```

```python
import jax
import jax.numpy as jnp
from jax import lax
from jax.experimental import pallas as pl
from jax.experimental.pallas import tpu as pltpu
from jax.sharding import PartitionSpec as P

MESH = pl.DeviceIdType.MESH
H = 4
DH = 32
ROWS = 8
COLS = 16
BF = jnp.bfloat16
F32 = jnp.float32
TRI, BACK, NORM, BIAS_COL, BIAS_ROW, BIAS_TWIN, HEADS = range(7)


def layer_norm(values, axis):
    center = values - jnp.mean(values, axis=axis, keepdims=True)
    spread = jnp.mean(center * center, axis=axis, keepdims=True)
    return center * lax.rsqrt(spread + 1e-05)


def nt(a, b):
    return lax.dot_general(a, b, (((1,), (1,)), ((), ())), preferred_element_type=F32)


def tn(a, b):
    return lax.dot_general(a, b, (((0,), (0,)), ((), ())), preferred_element_type=F32)


def nn(a, b):
    return lax.dot_general(a, b, (((1,), (0,)), ((), ())), preferred_element_type=F32)


def sigmoid(x):
    return 1.0 / (1.0 + jnp.exp(-x))


def lane_group(rows):
    return lax.broadcasted_iota(jnp.int32, (rows, 128), 1) // 32


def roll(x, shift):
    return x if shift % 128 == 0 else pltpu.roll(x, shift % 128, 1)


def block_kernel(
    lengths, pair_in, tri_in_in, tri_out_in, att_in_in, att_bias_in, att_out_in, out,
    pair, tri_in, tri_out, att_in, att_bias, att_out,
    tri_send, tri_got, back_send, back_got, norm_send, norm_got,
    bias_send, bias_got, bias_rows, bias_all, head_send, head_got,
    queries, keys, values, wide, gate, gate2, pair1, packed, gate_packed, out_packed, load_sem, send_sem, recv_sem, row_sem, twin_sem,
):
    row, col = lax.axis_index("row"), lax.axis_index("col")
    me = row * COLS + col

    loads = [
        pltpu.make_async_copy(src, dst, load_sem.at[n])
        for n, (src, dst) in enumerate(
            [
                (pair_in, pair), (tri_in_in, tri_in), (att_in_in, att_in),
                (att_out_in, att_out), (att_bias_in, att_bias), (tri_out_in, tri_out),
            ]
        )
    ]
    for load in loads:
        load.start()

    def anyone(t):
        return lax.rem(row + t // COLS, ROWS), lax.rem(col + lax.rem(t, COLS), COLS)

    def each(start, stop, body):
        def step(t, carry):
            body(t)
            return carry

        lax.fori_loop(start, stop, step, 0)

    def push(phase, src, dst, device, arrival=None):
        pltpu.make_async_remote_copy(
            src_ref=src, dst_ref=dst, send_sem=send_sem.at[phase],
            recv_sem=recv_sem.at[phase] if arrival is None else arrival,
            device_id=device, device_id_type=MESH,
        ).start()

    def landed(phase, ref):
        pltpu.make_async_copy(ref, ref, recv_sem.at[phase]).wait()

    def sent(phase, ref):
        pltpu.make_async_copy(ref, ref, send_sem.at[phase]).wait()

    barrier = pltpu.get_barrier_semaphore()

    def greet(t):
        pl.semaphore_signal(barrier, inc=1, device_id=anyone(t), device_id_type=MESH)

    each(1, ROWS * COLS, greet)

    loads[1].wait()
    columns = [tri_in[:, n * 128 : (n + 1) * 128] for n in range(5)]
    turned = [jnp.transpose(block.astype(F32)).astype(BF) for block in columns[:4]]
    weights = jnp.concatenate(
        [
            jnp.concatenate([turned[0], turned[2]], 1),
            jnp.concatenate([turned[1], turned[3]], 1),
        ],
        0,
    )
    lane = lax.broadcasted_iota(jnp.int32, (1, 128), 1)
    row_present = (lax.rem(lane, 64) < lengths[row]).astype(F32)
    col_length = lengths[col // 2] - lax.rem(col, 2) * 32
    zero = jnp.zeros((64, 128), BF)
    loads[0].wait()
    for k in range(32):
        norm = layer_norm(pair[:, k, :], 1).astype(BF)
        twin = jnp.concatenate(
            [jnp.concatenate([norm, zero], 1), jnp.concatenate([zero, norm], 1)], 0
        )
        both = nt(weights, twin)
        mask = row_present * jnp.where(k < col_length, 1.0, 0.0)
        wide[:, k, :] = sigmoid(both[:128]) * both[128:] * mask
    for c in range(0, 128, 16):
        tri_send[c : c + 16] = wide[c : c + 16].astype(BF)

    pl.semaphore_wait(barrier, ROWS * COLS - 1)

    def push_tri(t):
        r, c = anyone(t)
        push(TRI, tri_send.at[r * COLS + c], tri_got.at[me], (r, c))

    each(1, ROWS * COLS, push_tri)
    tri_got[me] = tri_send[me]

    for k in range(32):
        norm = layer_norm(pair[:, k, :], 1).astype(BF)
        gate[:, k, :] = sigmoid(nn(norm, columns[4]))
    for load in loads[2:]:
        load.wait()
    group = lane_group(128)
    mine_first = jnp.where(col // 8 == 0, 1.0, 0.0)
    for t in range(4):
        block = att_in[:, t * 128 : (t + 1) * 128].astype(F32)
        low = jnp.where(group < 2, block, 0.0)
        high = jnp.where(group < 2, 0.0, block)
        low_up, high_down = roll(low, 64), roll(high, 64)
        if t == 3:
            gate_packed[0:128, 0:128] = low.astype(BF)
            gate_packed[128:256, 0:128] = low_up.astype(BF)
            gate_packed[0:128, 128:256] = high_down.astype(BF)
            gate_packed[128:256, 128:256] = high.astype(BF)
        else:
            at = slice(t * 128, t * 128 + 128)
            packed[0:128, at] = jnp.where(mine_first > 0.5, low, high_down).astype(BF)
            packed[128:256, at] = jnp.where(mine_first > 0.5, low_up, high).astype(BF)
    out_packed[...] = jnp.zeros_like(out_packed)
    for p in range(2):
        for i in range(2):
            at = p * 128 + i * 64
            out_packed[at : at + 64, i * 128 : (i + 1) * 128] = att_out[p * 64 : p * 64 + 64, :]
    rest = att_bias[...]
    bias_weights = []
    for _ in range(3):
        part = rest.astype(BF)
        rest = rest - part.astype(F32)
        bias_weights.append(part)

    landed(TRI, tri_got.at[pl.ds(0, ROWS * COLS - 1)])
    group = lane_group(16)

    def product(r):
        left = tri_got[pl.ds(r * COLS, COLS)].reshape(512, 128)
        for s in range(ROWS):
            full = tn(left, tri_got[s * COLS : (s + 1) * COLS].reshape(512, 128))
            parts = [full[g * 16 : (g + 1) * 16] for g in range(4)]
            for half in range(2):
                packed_rows = None
                for g in range(4):
                    piece = roll(parts[g], g * 32 - 64 - half * 32)
                    packed_rows = piece if g == 0 else jnp.where(group == g, piece, packed_rows)
                back_send[r * COLS + s * 2 + half] = packed_rows.astype(BF)

    each(0, ROWS, product)

    def push_back(t):
        r, c = anyone(t)
        push(BACK, back_send.at[r * COLS + c], back_got.at[me], (r, c))

    each(1, ROWS * COLS, push_back)
    back_got[me] = back_send[me]
    landed(BACK, back_got.at[pl.ds(0, ROWS * COLS - 1)])

    for c in range(0, 128, 16):
        wide[c : c + 16, 0:16] = back_got[c : c + 16].astype(F32)
    for lo in range(16):
        update = tn(layer_norm(wide[:, lo, :], 0).astype(BF), tri_out[...])
        blocks = []
        for hi in range(4):
            i = hi * 16 + lo
            new = pair[i] + gate[i] * update[hi * 32 : (hi + 1) * 32]
            pair1[i] = new
            block = layer_norm(new, 1).astype(BF)
            at = (lo % 2) * 64 + (hi // 2) * 32
            norm_send[lo // 2, at : at + 32, (hi % 2) * 128 : (hi % 2) * 128 + 128] = block
            blocks.append(block)
        stacked = jnp.concatenate(blocks, 0)
        parts = [nt(w, stacked) for w in bias_weights]
        bias = parts[0] + (parts[1] + parts[2])
        for h in range(H):
            bias_send[h, lo : lo + 1, :] = bias[h : h + 1]

    def push_bias_col(t):
        c = lax.rem(col + t, COLS)
        push(BIAS_COL, bias_send.at[c // 8 * 2 + lax.rem(c, 2)], bias_got.at[col], (row, c))

    each(1, COLS, push_bias_col)
    head = lax.rem(col, 2)
    bias_got[col] = bias_send[col // 8 * 2 + head]

    def push_norm(t):
        c = lax.rem(col + t, COLS)
        push(NORM, norm_send.at[lax.rem(c, 8)], norm_got.at[col], (row, c))

    each(1, 5, push_norm)

    landed(BIAS_COL, bias_got.at[pl.ds(0, COLS - 1)])
    for hi in range(4):
        quads = []
        for quad in range(4):
            rows = None
            for q in range(4):
                piece = roll(bias_got[quad * 4 + q], q * 32 - hi * 32)
                rows = piece if q == 0 else jnp.where(group == q, piece, rows)
            length = jnp.where(lane < 64, lengths[quad * 2], lengths[quad * 2 + 1])
            quads.append(jnp.where(lax.rem(lane, 64) < length, rows, -1000000000.0))
        rows = jnp.concatenate(quads, 1)
        top = jnp.max(rows, axis=1, keepdims=True)
        bias_rows[hi * 16 : hi * 16 + 16] = (rows - top).astype(BF)
    bias_all[head, row] = bias_rows[...]

    def push_bias_row(t):
        r = lax.rem(row + t, ROWS)
        push(BIAS_ROW, bias_rows, bias_all.at[head, row], (r, col), row_sem.at[row])

    def push_twin(r):
        twin = bias_all.at[head, r]
        push(BIAS_TWIN, twin, twin, (row, col + 1 - 2 * head), twin_sem.at[r])

    push_twin(row)

    def push_both(t):
        push_bias_row(t)
        push_norm(2 * t + 3)
        push_norm(2 * t + 4)

    each(1, 6, push_both)
    push_bias_row(6)
    push_norm(15)
    push_bias_row(7)
    norm_got[col] = norm_send[lax.rem(col, 8)]

    for g in range(8):
        gate2[g] = sigmoid(nn(norm_send[g], gate_packed[...]))

    landed(NORM, norm_got.at[pl.ds(0, COLS - 1)])
    ones = jnp.ones((512, 128), BF)
    for n in range(4):
        normed = norm_got[:, n * 32 : n * 32 + 32, :].reshape(512, 256)
        queries[n] = (nn(normed, packed[:, 0:128]) * (DH ** (-0.5))).astype(BF)
        keys[n] = nn(normed, packed[:, 128:256]).astype(BF)
        values[n, :, 0:128] = nn(normed, packed[:, 256:384]).astype(BF)
        values[n, :, 128:256] = ones

    group = lane_group(64)

    def attend(r):
        pltpu.make_async_copy(bias_rows, bias_rows, twin_sem.at[r]).wait()
        at = pl.ds(pl.multiple_of(r * 64, 64), 64)

        def pair_of_rows(n):
            query = queries[n, at, :]
            mine = [jnp.where(group == g, query, jnp.zeros_like(query)) for g in range(4)]
            bias = [bias_all[0, r].astype(F32), bias_all[1, r].astype(F32)]
            score = nt(jnp.concatenate(mine, 0), keys[n]) + jnp.concatenate(bias + bias, 0)
            top = jnp.max(score, axis=1, keepdims=True)
            summed = nn(jnp.exp(score - top).astype(BF), values[n])
            result = summed[:, :128] / summed[:, 128:]
            total = result[0:64]
            for g in range(1, 4):
                total = jnp.where(group == g, result[g * 64 : g * 64 + 64], total)
            to = slice(n * 32, n * 32 + 32)
            head_send[2 * r, to, :] = total[:32].astype(BF)
            head_send[2 * r + 1, to, :] = total[32:].astype(BF)

        for n in range(4):
            pair_of_rows(n)
        for c in (2 * r, 2 * r + 1):

            @pl.when(c != col)
            def _():
                push(HEADS, head_send.at[c], head_got.at[col], (row, c))

    def attend_previous(t):
        @pl.when(t < ROWS)
        def _():
            r = lax.rem(row - t + ROWS, ROWS)
            pltpu.make_async_copy(bias_rows, bias_rows, row_sem.at[r]).wait()
            push_twin(r)

        attend(lax.rem(row - t + 1 + ROWS, ROWS))

    each(1, ROWS + 1, attend_previous)
    head_got[col] = head_send[col]
    landed(HEADS, head_got.at[pl.ds(0, COLS - 1)])

    for g in range(8):
        heads = jnp.concatenate([head_got[g], head_got[8 + g]], 1).astype(F32)
        result = nn((gate2[g] * heads).astype(BF), out_packed[...])
        for l in range(2):
            for hi in range(4):
                i = hi * 16 + g * 2 + l
                at = l * 64 + (hi // 2) * 32
                lanes = slice((hi % 2) * 128, (hi % 2) * 128 + 128)
                out[i] = pair1[i] + result[at : at + 32, lanes]

    sent(TRI, tri_send.at[pl.ds(0, ROWS * COLS - 1)])
    sent(BACK, back_send.at[pl.ds(0, ROWS * COLS - 1)])
    sent(NORM, norm_got.at[pl.ds(0, COLS - 1)])
    sent(BIAS_COL, bias_got.at[pl.ds(0, COLS - 1)])
    sent(BIAS_ROW, bias_all.at[0, pl.ds(0, ROWS - 1)])
    sent(BIAS_TWIN, bias_all.at[0])
    sent(HEADS, head_send.at[pl.ds(0, COLS - 1)])


def on_device(pair, chain_lengths, tri_in, tri_out, att_in, att_bias, att_out):
    vmem = pl.BlockSpec(memory_space=pltpu.VMEM)
    return pl.pallas_call(
        block_kernel,
        out_shape=jax.ShapeDtypeStruct((64, 32, 128), F32),
        in_specs=[pl.BlockSpec(memory_space=pltpu.SMEM)] + [pl.BlockSpec(memory_space=pltpu.HBM)] * 6,
        out_specs=vmem,
        scratch_shapes=[
            pltpu.VMEM((64, 32, 128), F32),
            pltpu.VMEM((128, 640), BF),
            pltpu.VMEM((128, 128), BF),
            pltpu.VMEM((128, 512), BF),
            pltpu.VMEM((4, 128), F32),
            pltpu.VMEM((128, 128), BF),
            pltpu.VMEM((128, 32, 128), BF),
            pltpu.VMEM((128, 32, 128), BF),
            pltpu.VMEM((128, 16, 128), BF),
            pltpu.VMEM((128, 16, 128), BF),
            pltpu.VMEM((8, 128, 256), BF),
            pltpu.VMEM((16, 128, 256), BF),
            pltpu.VMEM((4, 16, 128), F32),
            pltpu.VMEM((16, 16, 128), F32),
            pltpu.VMEM((64, 512), BF),
            pltpu.VMEM((2, 8, 64, 512), BF),
            pltpu.VMEM((16, 128, 128), BF),
            pltpu.VMEM((16, 128, 128), BF),
            pltpu.VMEM((4, 512, 128), BF),
            pltpu.VMEM((4, 512, 128), BF),
            pltpu.VMEM((4, 512, 256), BF),
            pltpu.VMEM((128, 32, 128), F32),
            pltpu.VMEM((64, 32, 128), F32),
            pltpu.VMEM((8, 128, 256), F32),
            pltpu.VMEM((64, 32, 128), F32),
            pltpu.VMEM((256, 384), BF),
            pltpu.VMEM((256, 256), BF),
            pltpu.VMEM((256, 256), BF),
            pltpu.SemaphoreType.DMA((6,)),
            pltpu.SemaphoreType.DMA((7,)),
            pltpu.SemaphoreType.DMA((7,)),
            pltpu.SemaphoreType.DMA((8,)),
            pltpu.SemaphoreType.DMA((8,)),
        ],
        name="pairformer",
        compiler_params=pltpu.CompilerParams(
            collective_id=0, has_side_effects=True, vmem_limit_bytes=63 << 20
        ),
    )(chain_lengths, pair, tri_in, tri_out, att_in, att_bias.T, att_out)


def solution(mesh):
    return jax.shard_map(
        on_device,
        mesh=mesh,
        in_specs=(P("row", "col", None), P(), P(), P(), P(), P(), P()),
        out_specs=P("row", "col", None),
        check_vma=False,
    )
```

```python
import jax
import jax.numpy as jnp
from jax import lax
from jax.experimental import pallas as pl
from jax.experimental.pallas import tpu as pltpu
from jax.sharding import PartitionSpec as P

MESH = pl.DeviceIdType.MESH
H = 4
DH = 32
ROWS = 8
COLS = 16
BF = jnp.bfloat16
F32 = jnp.float32
TRI, BACK, NORM, BIAS_COL, BIAS_ROW, BIAS_TWIN, HEADS = range(7)


def layer_norm(values, axis):
    center = values - jnp.mean(values, axis=axis, keepdims=True)
    spread = jnp.mean(center * center, axis=axis, keepdims=True)
    return center * lax.rsqrt(spread + 1e-05)


def nt(a, b):
    return lax.dot_general(a, b, (((1,), (1,)), ((), ())), preferred_element_type=F32)


def tn(a, b):
    return lax.dot_general(a, b, (((0,), (0,)), ((), ())), preferred_element_type=F32)


def nn(a, b):
    return lax.dot_general(a, b, (((1,), (0,)), ((), ())), preferred_element_type=F32)


def sigmoid(x):
    return 1.0 / (1.0 + jnp.exp(-x))


def lane_group(rows):
    return lax.broadcasted_iota(jnp.int32, (rows, 128), 1) // 32


def roll(x, shift):
    return x if shift % 128 == 0 else pltpu.roll(x, shift % 128, 1)


def block_kernel(
    lengths, pair_in, tri_in_in, tri_out_in, att_in_in, att_bias_in, att_out_in, out,
    pair, tri_in, tri_out, att_in, att_bias, att_out,
    tri_send, tri_got, back_send, back_got, norm_send, norm_got,
    bias_send, bias_got, bias_rows, bias_all, head_send, head_got,
    turned_left, queries, keys, values, wide, gate, gate2, pair1, packed, gate_packed, out_packed, load_sem, send_sem, recv_sem, tri_sem, row_sem, twin_sem,
):
    row, col = lax.axis_index("row"), lax.axis_index("col")
    me = row * COLS + col

    loads = [
        pltpu.make_async_copy(src, dst, load_sem.at[n])
        for n, (src, dst) in enumerate(
            [
                (pair_in, pair), (tri_in_in, tri_in), (att_in_in, att_in),
                (att_out_in, att_out), (att_bias_in, att_bias), (tri_out_in, tri_out),
            ]
        )
    ]
    for load in loads:
        load.start()

    def anyone(t):
        return lax.rem(row + t // COLS, ROWS), lax.rem(col + lax.rem(t, COLS), COLS)

    def each(start, stop, body):
        def step(t, carry):
            body(t)
            return carry

        lax.fori_loop(start, stop, step, 0)

    def push(phase, src, dst, device, arrival=None):
        pltpu.make_async_remote_copy(
            src_ref=src, dst_ref=dst, send_sem=send_sem.at[phase],
            recv_sem=recv_sem.at[phase] if arrival is None else arrival,
            device_id=device, device_id_type=MESH,
        ).start()

    def landed(phase, ref):
        pltpu.make_async_copy(ref, ref, recv_sem.at[phase]).wait()

    def sent(phase, ref):
        pltpu.make_async_copy(ref, ref, send_sem.at[phase]).wait()

    barrier = pltpu.get_barrier_semaphore()

    def greet(t):
        pl.semaphore_signal(barrier, inc=1, device_id=anyone(t), device_id_type=MESH)

    each(1, ROWS * COLS, greet)

    loads[1].wait()
    columns = [tri_in[:, n * 128 : (n + 1) * 128] for n in range(5)]
    turned = [jnp.transpose(block.astype(F32)).astype(BF) for block in columns[:4]]
    weights = jnp.concatenate(
        [
            jnp.concatenate([turned[0], turned[2]], 1),
            jnp.concatenate([turned[1], turned[3]], 1),
        ],
        0,
    )
    lane = lax.broadcasted_iota(jnp.int32, (1, 128), 1)
    row_present = (lax.rem(lane, 64) < lengths[row]).astype(F32)
    col_length = lengths[col // 2] - lax.rem(col, 2) * 32
    zero = jnp.zeros((64, 128), BF)
    loads[0].wait()
    for k in range(32):
        norm = layer_norm(pair[:, k, :], 1).astype(BF)
        twin = jnp.concatenate(
            [jnp.concatenate([norm, zero], 1), jnp.concatenate([zero, norm], 1)], 0
        )
        both = nt(weights, twin)
        mask = row_present * jnp.where(k < col_length, 1.0, 0.0)
        wide[:, k, :] = sigmoid(both[:128]) * both[128:] * mask
    for c in range(0, 128, 16):
        tri_send[c : c + 16] = wide[c : c + 16].astype(BF)

    pl.semaphore_wait(barrier, ROWS * COLS - 1)

    def push_tri(t):
        r, c = anyone(t)
        push(TRI, tri_send.at[r * COLS + c], tri_got.at[me], (r, c), tri_sem.at[row])

    each(1, ROWS * COLS, push_tri)
    tri_got[me] = tri_send[me]

    for k in range(32):
        norm = layer_norm(pair[:, k, :], 1).astype(BF)
        gate[:, k, :] = sigmoid(nn(norm, columns[4]))
    for load in loads[2:]:
        load.wait()
    group = lane_group(128)
    mine_first = jnp.where(col // 8 == 0, 1.0, 0.0)
    for t in range(4):
        block = att_in[:, t * 128 : (t + 1) * 128].astype(F32)
        low = jnp.where(group < 2, block, 0.0)
        high = jnp.where(group < 2, 0.0, block)
        low_up, high_down = roll(low, 64), roll(high, 64)
        if t == 3:
            gate_packed[0:128, 0:128] = low.astype(BF)
            gate_packed[128:256, 0:128] = low_up.astype(BF)
            gate_packed[0:128, 128:256] = high_down.astype(BF)
            gate_packed[128:256, 128:256] = high.astype(BF)
        else:
            at = slice(t * 128, t * 128 + 128)
            packed[0:128, at] = jnp.where(mine_first > 0.5, low, high_down).astype(BF)
            packed[128:256, at] = jnp.where(mine_first > 0.5, low_up, high).astype(BF)
    out_packed[...] = jnp.zeros_like(out_packed)
    for p in range(2):
        for i in range(2):
            at = p * 128 + i * 64
            out_packed[at : at + 64, i * 128 : (i + 1) * 128] = att_out[p * 64 : p * 64 + 64, :]
    rest = att_bias[...]
    bias_weights = []
    for _ in range(3):
        part = rest.astype(BF)
        rest = rest - part.astype(F32)
        bias_weights.append(part)

    group = lane_group(16)

    def near(distance):
        return lax.rem(row - distance + ROWS, ROWS)

    def product(r, s):
        full = nn(turned_left[r], tri_got[pl.ds(s * COLS, COLS)].reshape(512, 128))
        parts = [full[g * 16 : (g + 1) * 16] for g in range(4)]
        for half in range(2):
            packed_rows = None
            for g in range(4):
                piece = roll(parts[g], g * 32 - 64 - half * 32)
                packed_rows = piece if g == 0 else jnp.where(group == g, piece, packed_rows)
            back_send[r * COLS + s * 2 + half] = packed_rows.astype(BF)

    def push_back(r, c):
        @pl.when(r * COLS + c != me)
        def _():
            push(BACK, back_send.at[r * COLS + c], back_got.at[me], (r, c))

    for distance in range(ROWS):
        new = near(distance)
        arrived = tri_got.at[pl.ds(0, COLS - 1 if distance == 0 else COLS)]
        pltpu.make_async_copy(arrived, arrived, tri_sem.at[new]).wait()
        got = tri_got[pl.ds(new * COLS, COLS)].reshape(512, 128)
        turned_left[new] = jnp.transpose(got.astype(F32))[:64].astype(BF)
        product(new, new)
        for older in range(distance):
            product(new, near(older))
            product(near(older), new)

        def push_new(older):
            push_back(new, near(older) * 2)
            push_back(new, near(older) * 2 + 1)

        def push_older(older):
            push_back(near(older), new * 2)
            push_back(near(older), new * 2 + 1)

        each(0, distance + 1, push_new)
        each(0, distance, push_older)
    back_got[me] = back_send[me]
    landed(BACK, back_got.at[pl.ds(0, ROWS * COLS - 1)])

    for c in range(0, 128, 16):
        wide[c : c + 16, 0:16] = back_got[c : c + 16].astype(F32)
    for lo in range(16):
        update = tn(layer_norm(wide[:, lo, :], 0).astype(BF), tri_out[...])
        blocks = []
        for hi in range(4):
            i = hi * 16 + lo
            new = pair[i] + gate[i] * update[hi * 32 : (hi + 1) * 32]
            pair1[i] = new
            block = layer_norm(new, 1).astype(BF)
            at = (lo % 2) * 64 + (hi // 2) * 32
            norm_send[lo // 2, at : at + 32, (hi % 2) * 128 : (hi % 2) * 128 + 128] = block
            blocks.append(block)
        stacked = jnp.concatenate(blocks, 0)
        parts = [nt(w, stacked) for w in bias_weights]
        bias = parts[0] + (parts[1] + parts[2])
        for h in range(H):
            bias_send[h, lo : lo + 1, :] = bias[h : h + 1]

    def push_bias_col(t):
        c = lax.rem(col + t, COLS)
        push(BIAS_COL, bias_send.at[c // 8 * 2 + lax.rem(c, 2)], bias_got.at[col], (row, c))

    each(1, COLS, push_bias_col)
    head = lax.rem(col, 2)
    bias_got[col] = bias_send[col // 8 * 2 + head]

    def push_norm(t):
        c = lax.rem(col + t, COLS)
        push(NORM, norm_send.at[lax.rem(c, 8)], norm_got.at[col], (row, c))

    each(1, 5, push_norm)

    landed(BIAS_COL, bias_got.at[pl.ds(0, COLS - 1)])
    for hi in range(4):
        quads = []
        for quad in range(4):
            rows = None
            for q in range(4):
                piece = roll(bias_got[quad * 4 + q], q * 32 - hi * 32)
                rows = piece if q == 0 else jnp.where(group == q, piece, rows)
            length = jnp.where(lane < 64, lengths[quad * 2], lengths[quad * 2 + 1])
            quads.append(jnp.where(lax.rem(lane, 64) < length, rows, -1000000000.0))
        rows = jnp.concatenate(quads, 1)
        top = jnp.max(rows, axis=1, keepdims=True)
        bias_rows[hi * 16 : hi * 16 + 16] = (rows - top).astype(BF)
    bias_all[head, row] = bias_rows[...]

    def push_bias_row(t):
        r = lax.rem(row + t, ROWS)
        push(BIAS_ROW, bias_rows, bias_all.at[head, row], (r, col), row_sem.at[row])

    def push_twin(r):
        twin = bias_all.at[head, r]
        push(BIAS_TWIN, twin, twin, (row, col + 1 - 2 * head), twin_sem.at[r])

    push_twin(row)

    def push_both(t):
        push_bias_row(t)
        push_norm(2 * t + 3)
        push_norm(2 * t + 4)

    each(1, 6, push_both)
    push_bias_row(6)
    push_norm(15)
    push_bias_row(7)
    norm_got[col] = norm_send[lax.rem(col, 8)]

    for g in range(8):
        gate2[g] = sigmoid(nn(norm_send[g], gate_packed[...]))

    landed(NORM, norm_got.at[pl.ds(0, COLS - 1)])
    ones = jnp.ones((512, 128), BF)
    for n in range(4):
        normed = norm_got[:, n * 32 : n * 32 + 32, :].reshape(512, 256)
        queries[n] = (nn(normed, packed[:, 0:128]) * (DH ** (-0.5))).astype(BF)
        keys[n] = nn(normed, packed[:, 128:256]).astype(BF)
        values[n, :, 0:128] = nn(normed, packed[:, 256:384]).astype(BF)
        values[n, :, 128:256] = ones

    group = lane_group(64)

    def attend(r):
        pltpu.make_async_copy(bias_rows, bias_rows, twin_sem.at[r]).wait()
        at = pl.ds(pl.multiple_of(r * 64, 64), 64)

        def pair_of_rows(n):
            query = queries[n, at, :]
            mine = [jnp.where(group == g, query, jnp.zeros_like(query)) for g in range(4)]
            bias = [bias_all[0, r].astype(F32), bias_all[1, r].astype(F32)]
            score = nt(jnp.concatenate(mine, 0), keys[n]) + jnp.concatenate(bias + bias, 0)
            top = jnp.max(score, axis=1, keepdims=True)
            summed = nn(jnp.exp(score - top).astype(BF), values[n])
            result = summed[:, :128] / summed[:, 128:]
            total = result[0:64]
            for g in range(1, 4):
                total = jnp.where(group == g, result[g * 64 : g * 64 + 64], total)
            to = slice(n * 32, n * 32 + 32)
            head_send[2 * r, to, :] = total[:32].astype(BF)
            head_send[2 * r + 1, to, :] = total[32:].astype(BF)

        for n in range(4):
            pair_of_rows(n)
        for c in (2 * r, 2 * r + 1):

            @pl.when(c != col)
            def _():
                push(HEADS, head_send.at[c], head_got.at[col], (row, c))

    def attend_previous(t):
        @pl.when(t < ROWS)
        def _():
            r = lax.rem(row - t + ROWS, ROWS)
            pltpu.make_async_copy(bias_rows, bias_rows, row_sem.at[r]).wait()
            push_twin(r)

        attend(lax.rem(row - t + 1 + ROWS, ROWS))

    each(1, ROWS + 1, attend_previous)
    head_got[col] = head_send[col]
    landed(HEADS, head_got.at[pl.ds(0, COLS - 1)])

    for g in range(8):
        heads = jnp.concatenate([head_got[g], head_got[8 + g]], 1).astype(F32)
        result = nn((gate2[g] * heads).astype(BF), out_packed[...])
        for l in range(2):
            for hi in range(4):
                i = hi * 16 + g * 2 + l
                at = l * 64 + (hi // 2) * 32
                lanes = slice((hi % 2) * 128, (hi % 2) * 128 + 128)
                out[i] = pair1[i] + result[at : at + 32, lanes]

    sent(TRI, tri_send.at[pl.ds(0, ROWS * COLS - 1)])
    sent(BACK, back_send.at[pl.ds(0, ROWS * COLS - 1)])
    sent(NORM, norm_got.at[pl.ds(0, COLS - 1)])
    sent(BIAS_COL, bias_got.at[pl.ds(0, COLS - 1)])
    sent(BIAS_ROW, bias_all.at[0, pl.ds(0, ROWS - 1)])
    sent(BIAS_TWIN, bias_all.at[0])
    sent(HEADS, head_send.at[pl.ds(0, COLS - 1)])


def on_device(pair, chain_lengths, tri_in, tri_out, att_in, att_bias, att_out):
    vmem = pl.BlockSpec(memory_space=pltpu.VMEM)
    return pl.pallas_call(
        block_kernel,
        out_shape=jax.ShapeDtypeStruct((64, 32, 128), F32),
        in_specs=[pl.BlockSpec(memory_space=pltpu.SMEM)] + [pl.BlockSpec(memory_space=pltpu.HBM)] * 6,
        out_specs=vmem,
        scratch_shapes=[
            pltpu.VMEM((64, 32, 128), F32),
            pltpu.VMEM((128, 640), BF),
            pltpu.VMEM((128, 128), BF),
            pltpu.VMEM((128, 512), BF),
            pltpu.VMEM((4, 128), F32),
            pltpu.VMEM((128, 128), BF),
            pltpu.VMEM((128, 32, 128), BF),
            pltpu.VMEM((128, 32, 128), BF),
            pltpu.VMEM((128, 16, 128), BF),
            pltpu.VMEM((128, 16, 128), BF),
            pltpu.VMEM((8, 128, 256), BF),
            pltpu.VMEM((16, 128, 256), BF),
            pltpu.VMEM((4, 16, 128), F32),
            pltpu.VMEM((16, 16, 128), F32),
            pltpu.VMEM((64, 512), BF),
            pltpu.VMEM((2, 8, 64, 512), BF),
            pltpu.VMEM((16, 128, 128), BF),
            pltpu.VMEM((16, 128, 128), BF),
            pltpu.VMEM((8, 64, 512), BF),
            pltpu.VMEM((4, 512, 128), BF),
            pltpu.VMEM((4, 512, 128), BF),
            pltpu.VMEM((4, 512, 256), BF),
            pltpu.VMEM((128, 32, 128), F32),
            pltpu.VMEM((64, 32, 128), F32),
            pltpu.VMEM((8, 128, 256), F32),
            pltpu.VMEM((64, 32, 128), F32),
            pltpu.VMEM((256, 384), BF),
            pltpu.VMEM((256, 256), BF),
            pltpu.VMEM((256, 256), BF),
            pltpu.SemaphoreType.DMA((6,)),
            pltpu.SemaphoreType.DMA((7,)),
            pltpu.SemaphoreType.DMA((7,)),
            pltpu.SemaphoreType.DMA((8,)),
            pltpu.SemaphoreType.DMA((8,)),
            pltpu.SemaphoreType.DMA((8,)),
        ],
        name="pairformer",
        compiler_params=pltpu.CompilerParams(
            collective_id=0, has_side_effects=True, vmem_limit_bytes=63 << 20
        ),
    )(chain_lengths, pair, tri_in, tri_out, att_in, att_bias.T, att_out)


def solution(mesh):
    return jax.shard_map(
        on_device,
        mesh=mesh,
        in_specs=(P("row", "col", None), P(), P(), P(), P(), P(), P()),
        out_specs=P("row", "col", None),
        check_vma=False,
    )
```

```python
import jax
import jax.numpy as jnp
from jax import lax
from jax.experimental import pallas as pl
from jax.experimental.pallas import tpu as pltpu
from jax.sharding import PartitionSpec as P

MESH = pl.DeviceIdType.MESH
H = 4
DH = 32
ROWS = 8
COLS = 16
BF = jnp.bfloat16
F32 = jnp.float32
TRI, BACK, NORM, NORM_TWIN, BIAS_COL, BIAS_ROW, HEADS = range(7)


def layer_norm(values, axis):
    center = values - jnp.mean(values, axis=axis, keepdims=True)
    spread = jnp.mean(center * center, axis=axis, keepdims=True)
    return center * lax.rsqrt(spread + 1e-05)


def nt(a, b):
    return lax.dot_general(a, b, (((1,), (1,)), ((), ())), preferred_element_type=F32)


def tn(a, b):
    return lax.dot_general(a, b, (((0,), (0,)), ((), ())), preferred_element_type=F32)


def nn(a, b):
    return lax.dot_general(a, b, (((1,), (0,)), ((), ())), preferred_element_type=F32)


def sigmoid(x):
    return 1.0 / (1.0 + jnp.exp(-x))


def lane_group(rows):
    return lax.broadcasted_iota(jnp.int32, (rows, 128), 1) // 32


def roll(x, shift):
    return x if shift % 128 == 0 else pltpu.roll(x, shift % 128, 1)


def block_kernel(
    lengths, pair_in, tri_in_in, tri_out_in, att_in_in, att_bias_in, att_out_in, out,
    pair, tri_in, tri_out, att_in, att_bias, att_out,
    tri_send, tri_got, back_send, back_got, norm_send, norm_got,
    bias_send, bias_got, bias_rows, bias_all, head_send, head_got,
    turned_left, queries, keys, values, wide, gate, gate2, pair1, packed, gate_packed, out_packed, load_sem, send_sem, recv_sem, tri_sem, row_sem,
):
    row, col = lax.axis_index("row"), lax.axis_index("col")
    me = row * COLS + col
    core = lax.rem(col, 2)

    loads = [
        pltpu.make_async_copy(src, dst, load_sem.at[n])
        for n, (src, dst) in enumerate(
            [
                (pair_in, pair), (tri_in_in, tri_in), (att_in_in, att_in),
                (att_out_in, att_out), (att_bias_in, att_bias), (tri_out_in, tri_out),
            ]
        )
    ]
    for load in loads:
        load.start()

    def anyone(t):
        return lax.rem(row + t // COLS, ROWS), lax.rem(col + lax.rem(t, COLS), COLS)

    def each(start, stop, body):
        def step(t, carry):
            body(t)
            return carry

        lax.fori_loop(start, stop, step, 0)

    def push(phase, src, dst, device, arrival=None):
        pltpu.make_async_remote_copy(
            src_ref=src, dst_ref=dst, send_sem=send_sem.at[phase],
            recv_sem=recv_sem.at[phase] if arrival is None else arrival,
            device_id=device, device_id_type=MESH,
        ).start()

    def landed(phase, ref):
        pltpu.make_async_copy(ref, ref, recv_sem.at[phase]).wait()

    def sent(phase, ref):
        pltpu.make_async_copy(ref, ref, send_sem.at[phase]).wait()

    barrier = pltpu.get_barrier_semaphore()

    def greet(t):
        pl.semaphore_signal(barrier, inc=1, device_id=anyone(t), device_id_type=MESH)

    each(1, ROWS * COLS, greet)

    loads[1].wait()
    columns = [tri_in[:, n * 128 : (n + 1) * 128] for n in range(5)]
    turned = [jnp.transpose(block.astype(F32)).astype(BF) for block in columns[:4]]
    weights = jnp.concatenate(
        [
            jnp.concatenate([turned[0], turned[2]], 1),
            jnp.concatenate([turned[1], turned[3]], 1),
        ],
        0,
    )
    lane = lax.broadcasted_iota(jnp.int32, (1, 128), 1)
    row_present = (lax.rem(lane, 64) < lengths[row]).astype(F32)
    col_length = lengths[col // 2] - lax.rem(col, 2) * 32
    zero = jnp.zeros((64, 128), BF)
    loads[0].wait()
    for k in range(32):
        norm = layer_norm(pair[:, k, :], 1).astype(BF)
        twin = jnp.concatenate(
            [jnp.concatenate([norm, zero], 1), jnp.concatenate([zero, norm], 1)], 0
        )
        both = nt(weights, twin)
        mask = row_present * jnp.where(k < col_length, 1.0, 0.0)
        wide[:, k, :] = sigmoid(both[:128]) * both[128:] * mask
    for c in range(0, 128, 16):
        tri_send[c : c + 16] = wide[c : c + 16].astype(BF)

    pl.semaphore_wait(barrier, ROWS * COLS - 1)

    def push_tri(t):
        r, c = anyone(t)
        push(TRI, tri_send.at[r * COLS + c], tri_got.at[me], (r, c), tri_sem.at[row])

    each(1, ROWS * COLS, push_tri)
    tri_got[me] = tri_send[me]

    for k in range(32):
        norm = layer_norm(pair[:, k, :], 1).astype(BF)
        gate[:, k, :] = sigmoid(nn(norm, columns[4]))
    for load in loads[2:]:
        load.wait()
    group = lane_group(128)
    mine_first = jnp.where(core == 0, 1.0, 0.0)
    for t in range(4):
        block = att_in[:, t * 128 : (t + 1) * 128].astype(F32)
        low = jnp.where(group < 2, block, 0.0)
        high = jnp.where(group < 2, 0.0, block)
        low_up, high_down = roll(low, 64), roll(high, 64)
        if t == 3:
            gate_packed[0:128, 0:128] = low.astype(BF)
            gate_packed[128:256, 0:128] = low_up.astype(BF)
            gate_packed[0:128, 128:256] = high_down.astype(BF)
            gate_packed[128:256, 128:256] = high.astype(BF)
        else:
            at = slice(t * 128, t * 128 + 128)
            packed[0:128, at] = jnp.where(mine_first > 0.5, low, high_down).astype(BF)
            packed[128:256, at] = jnp.where(mine_first > 0.5, low_up, high).astype(BF)
    out_packed[...] = jnp.zeros_like(out_packed)
    for p in range(2):
        for i in range(2):
            at = p * 128 + i * 64
            out_packed[at : at + 64, i * 128 : (i + 1) * 128] = att_out[p * 64 : p * 64 + 64, :]
    rest = att_bias[...]
    bias_weights = []
    for _ in range(3):
        part = rest.astype(BF)
        rest = rest - part.astype(F32)
        bias_weights.append(part)

    group = lane_group(16)

    def near(distance):
        return lax.rem(row - distance + ROWS, ROWS)

    def product(r, s):
        full = nn(turned_left[r], tri_got[pl.ds(s * COLS, COLS)].reshape(512, 128))
        parts = [full[g * 16 : (g + 1) * 16] for g in range(4)]
        for half in range(2):
            packed_rows = None
            for g in range(4):
                piece = roll(parts[g], g * 32 - 64 - half * 32)
                packed_rows = piece if g == 0 else jnp.where(group == g, piece, packed_rows)
            back_send[r * COLS + s * 2 + half] = packed_rows.astype(BF)

    def push_back(r, c):
        @pl.when(r * COLS + c != me)
        def _():
            push(BACK, back_send.at[r * COLS + c], back_got.at[me], (r, c))

    for distance in range(ROWS):
        new = near(distance)
        arrived = tri_got.at[pl.ds(0, COLS - 1 if distance == 0 else COLS)]
        pltpu.make_async_copy(arrived, arrived, tri_sem.at[new]).wait()
        got = tri_got[pl.ds(new * COLS, COLS)].reshape(512, 128)
        turned_left[new] = jnp.transpose(got.astype(F32))[:64].astype(BF)
        product(new, new)
        for older in range(distance):
            product(new, near(older))
            product(near(older), new)

        def push_new(older):
            push_back(new, near(older) * 2)
            push_back(new, near(older) * 2 + 1)

        def push_older(older):
            push_back(near(older), new * 2)
            push_back(near(older), new * 2 + 1)

        each(0, distance + 1, push_new)
        each(0, distance, push_older)
    back_got[me] = back_send[me]
    landed(BACK, back_got.at[pl.ds(0, ROWS * COLS - 1)])

    for c in range(0, 128, 16):
        wide[c : c + 16, 0:16] = back_got[c : c + 16].astype(F32)
    for lo in range(16):
        update = tn(layer_norm(wide[:, lo, :], 0).astype(BF), tri_out[...])
        blocks = []
        for hi in range(4):
            i = hi * 16 + lo
            new = pair[i] + gate[i] * update[hi * 32 : (hi + 1) * 32]
            pair1[i] = new
            block = layer_norm(new, 1).astype(BF)
            at = (lo % 2) * 64 + (hi // 2) * 32
            norm_send[lo // 2, at : at + 32, (hi % 2) * 128 : (hi % 2) * 128 + 128] = block
            blocks.append(block)
        stacked = jnp.concatenate(blocks, 0)
        parts = [nt(w, stacked) for w in bias_weights]
        bias = parts[0] + (parts[1] + parts[2])
        for h in range(H):
            bias_send[h, lo : lo + 1, :] = bias[h : h + 1]

    def push_bias_col(t):
        c = lax.rem(col + t, COLS)
        heads = bias_send.at[pl.ds(lax.rem(c, 2) * 2, 2)]
        push(BIAS_COL, heads, bias_got.at[col], (row, c))

    each(1, COLS, push_bias_col)
    bias_got[col] = bias_send[pl.ds(core * 2, 2)]

    def push_norm(t):
        g = lax.rem(col // 2 + t, 8)
        push(NORM, norm_send.at[g], norm_got.at[core, col // 2], (row, g * 2 + core))

    each(1, 4, push_norm)
    norm_got[core, col // 2] = norm_send[col // 2]

    landed(BIAS_COL, bias_got.at[pl.ds(0, COLS - 1)])
    for h in range(2):
        for hi in range(4):
            quads = []
            for quad in range(4):
                rows = None
                for q in range(4):
                    piece = roll(bias_got[quad * 4 + q, h], q * 32 - hi * 32)
                    rows = piece if q == 0 else jnp.where(group == q, piece, rows)
                length = jnp.where(lane < 64, lengths[quad * 2], lengths[quad * 2 + 1])
                quads.append(jnp.where(lax.rem(lane, 64) < length, rows, -1000000000.0))
            rows = jnp.concatenate(quads, 1)
            top = jnp.max(rows, axis=1, keepdims=True)
            bias_rows[h, hi * 16 : hi * 16 + 16] = (rows - top).astype(BF)
    bias_all[row] = bias_rows[...]

    def differ(a, b):
        return a + b - 2 * a * b

    def partner(t):
        flip = 3 - (t - 1) // 2
        low = differ(lax.rem(row, 2), flip % 2)
        high = differ(lax.rem(row // 2, 2), flip // 2)
        return low + 2 * high + 4 * differ(row // 4, 1 - t % 2 + t // 7)

    def push_bias_row(t):
        push(BIAS_ROW, bias_rows, bias_all.at[row], (partner(t), col), row_sem.at[row])

    for t in range(1, 5):
        push_bias_row(t)
        push_norm(t + 3)
    for t in range(5, ROWS):
        push_bias_row(t)

    for g in range(8):
        gate2[g] = sigmoid(nn(norm_send[g], gate_packed[...]))

    landed(NORM, norm_got.at[0, pl.ds(0, 7)])
    twin = norm_got.at[core]
    push(NORM_TWIN, twin, twin, (row, col + 1 - 2 * core))
    landed(NORM_TWIN, norm_got.at[0])
    ones = jnp.ones((512, 128), BF)
    for n in range(4):
        normed = jnp.swapaxes(norm_got[:, :, n * 32 : n * 32 + 32, :], 0, 1).reshape(512, 256)
        queries[n] = (nn(normed, packed[:, 0:128]) * (DH ** (-0.5))).astype(BF)
        keys[n] = nn(normed, packed[:, 128:256]).astype(BF)
        values[n, :, 0:128] = nn(normed, packed[:, 256:384]).astype(BF)
        values[n, :, 128:256] = ones

    group = lane_group(64)

    def attend(r):
        at = pl.ds(pl.multiple_of(r * 64, 64), 64)

        def pair_of_rows(n):
            query = queries[n, at, :]
            mine = [jnp.where(group == g, query, jnp.zeros_like(query)) for g in range(4)]
            bias = [bias_all[r, 0].astype(F32), bias_all[r, 1].astype(F32)]
            score = nt(jnp.concatenate(mine, 0), keys[n]) + jnp.concatenate(bias + bias, 0)
            top = jnp.max(score, axis=1, keepdims=True)
            summed = nn(jnp.exp(score - top).astype(BF), values[n])
            result = summed[:, :128] / summed[:, 128:]
            total = result[0:64]
            for g in range(1, 4):
                total = jnp.where(group == g, result[g * 64 : g * 64 + 64], total)
            to = slice(n * 32, n * 32 + 32)
            head_send[2 * r, to, :] = total[:32].astype(BF)
            head_send[2 * r + 1, to, :] = total[32:].astype(BF)

        for n in range(4):
            pair_of_rows(n)
        for c in (2 * r, 2 * r + 1):

            @pl.when(c != col)
            def _():
                push(HEADS, head_send.at[c], head_got.at[col], (row, c))

    attend(row)

    def attend_next(t):
        r = partner(t)
        pltpu.make_async_copy(bias_rows, bias_rows, row_sem.at[r]).wait()
        attend(r)

    each(1, ROWS, attend_next)
    head_got[col] = head_send[col]
    landed(HEADS, head_got.at[pl.ds(0, COLS - 1)])

    for g in range(8):
        heads = jnp.concatenate([head_got[2 * g], head_got[2 * g + 1]], 1).astype(F32)
        result = nn((gate2[g] * heads).astype(BF), out_packed[...])
        for l in range(2):
            for hi in range(4):
                i = hi * 16 + g * 2 + l
                at = l * 64 + (hi // 2) * 32
                lanes = slice((hi % 2) * 128, (hi % 2) * 128 + 128)
                out[i] = pair1[i] + result[at : at + 32, lanes]

    sent(TRI, tri_send.at[pl.ds(0, ROWS * COLS - 1)])
    sent(BACK, back_send.at[pl.ds(0, ROWS * COLS - 1)])
    sent(NORM, norm_got.at[0, pl.ds(0, 7)])
    sent(NORM_TWIN, norm_got.at[0])
    sent(BIAS_COL, bias_got.at[pl.ds(0, COLS - 1)])
    sent(BIAS_ROW, bias_all.at[pl.ds(0, ROWS - 1)])
    sent(HEADS, head_send.at[pl.ds(0, COLS - 1)])


def on_device(pair, chain_lengths, tri_in, tri_out, att_in, att_bias, att_out):
    vmem = pl.BlockSpec(memory_space=pltpu.VMEM)
    return pl.pallas_call(
        block_kernel,
        out_shape=jax.ShapeDtypeStruct((64, 32, 128), F32),
        in_specs=[pl.BlockSpec(memory_space=pltpu.SMEM)] + [pl.BlockSpec(memory_space=pltpu.HBM)] * 6,
        out_specs=vmem,
        scratch_shapes=[
            pltpu.VMEM((64, 32, 128), F32),
            pltpu.VMEM((128, 640), BF),
            pltpu.VMEM((128, 128), BF),
            pltpu.VMEM((128, 512), BF),
            pltpu.VMEM((4, 128), F32),
            pltpu.VMEM((128, 128), BF),
            pltpu.VMEM((128, 32, 128), BF),
            pltpu.VMEM((128, 32, 128), BF),
            pltpu.VMEM((128, 16, 128), BF),
            pltpu.VMEM((128, 16, 128), BF),
            pltpu.VMEM((8, 128, 256), BF),
            pltpu.VMEM((2, 8, 128, 256), BF),
            pltpu.VMEM((4, 16, 128), F32),
            pltpu.VMEM((16, 2, 16, 128), F32),
            pltpu.VMEM((2, 64, 512), BF),
            pltpu.VMEM((8, 2, 64, 512), BF),
            pltpu.VMEM((16, 128, 128), BF),
            pltpu.VMEM((16, 128, 128), BF),
            pltpu.VMEM((8, 64, 512), BF),
            pltpu.VMEM((4, 512, 128), BF),
            pltpu.VMEM((4, 512, 128), BF),
            pltpu.VMEM((4, 512, 256), BF),
            pltpu.VMEM((128, 32, 128), F32),
            pltpu.VMEM((64, 32, 128), F32),
            pltpu.VMEM((8, 128, 256), F32),
            pltpu.VMEM((64, 32, 128), F32),
            pltpu.VMEM((256, 384), BF),
            pltpu.VMEM((256, 256), BF),
            pltpu.VMEM((256, 256), BF),
            pltpu.SemaphoreType.DMA((6,)),
            pltpu.SemaphoreType.DMA((7,)),
            pltpu.SemaphoreType.DMA((7,)),
            pltpu.SemaphoreType.DMA((8,)),
            pltpu.SemaphoreType.DMA((8,)),
        ],
        name="pairformer",
        compiler_params=pltpu.CompilerParams(
            collective_id=0, has_side_effects=True, vmem_limit_bytes=63 << 20
        ),
    )(chain_lengths, pair, tri_in, tri_out, att_in, att_bias.T, att_out)


def solution(mesh):
    return jax.shard_map(
        on_device,
        mesh=mesh,
        in_specs=(P("row", "col", None), P(), P(), P(), P(), P(), P()),
        out_specs=P("row", "col", None),
        check_vma=False,
    )
```

```python
import jax
import jax.numpy as jnp
from jax import lax
from jax.experimental import pallas as pl
from jax.experimental.pallas import tpu as pltpu
from jax.sharding import PartitionSpec as P

MESH = pl.DeviceIdType.MESH
H = 4
DH = 32
ROWS = 8
COLS = 16
BF = jnp.bfloat16
F32 = jnp.float32
TRI, BACK, NORM, NORM_TWIN, BIAS_COL, BIAS_ROW, HEADS = range(7)


def layer_norm(values, axis):
    center = values - jnp.mean(values, axis=axis, keepdims=True)
    spread = jnp.mean(center * center, axis=axis, keepdims=True)
    return center * lax.rsqrt(spread + 1e-05)


def nt(a, b):
    return lax.dot_general(a, b, (((1,), (1,)), ((), ())), preferred_element_type=F32)


def tn(a, b):
    return lax.dot_general(a, b, (((0,), (0,)), ((), ())), preferred_element_type=F32)


def nn(a, b):
    return lax.dot_general(a, b, (((1,), (0,)), ((), ())), preferred_element_type=F32)


def sigmoid(x):
    return 1.0 / (1.0 + jnp.exp(-x))


def lane_group(rows):
    return lax.broadcasted_iota(jnp.int32, (rows, 128), 1) // 32


def roll(x, shift):
    return x if shift % 128 == 0 else pltpu.roll(x, shift % 128, 1)


def block_kernel(
    lengths, pair_in, tri_in_in, tri_out_in, att_in_in, att_bias_in, att_out_in, out,
    pair, tri_in, tri_out, att_in, att_bias, att_out,
    tri_send, tri_got, back_send, back_got, norm_send, norm_got,
    bias_send, bias_got, bias_rows, bias_all, head_send, head_got,
    turned_left, queries, keys, values, wide, gate, gate2, pair1, packed, gate_packed, out_packed, load_sem, send_sem, recv_sem, tri_sem, norm_sem, row_sem,
):
    row, col = lax.axis_index("row"), lax.axis_index("col")
    me = row * COLS + col
    core = lax.rem(col, 2)

    loads = [
        pltpu.make_async_copy(src, dst, load_sem.at[n])
        for n, (src, dst) in enumerate(
            [
                (pair_in, pair), (tri_in_in, tri_in), (att_in_in, att_in),
                (att_out_in, att_out), (att_bias_in, att_bias), (tri_out_in, tri_out),
            ]
        )
    ]
    for load in loads:
        load.start()

    def anyone(t):
        return lax.rem(row + t // COLS, ROWS), lax.rem(col + lax.rem(t, COLS), COLS)

    def each(start, stop, body):
        def step(t, carry):
            body(t)
            return carry

        lax.fori_loop(start, stop, step, 0)

    def push(phase, src, dst, device, arrival=None):
        pltpu.make_async_remote_copy(
            src_ref=src, dst_ref=dst, send_sem=send_sem.at[phase],
            recv_sem=recv_sem.at[phase] if arrival is None else arrival,
            device_id=device, device_id_type=MESH,
        ).start()

    def landed(phase, ref):
        pltpu.make_async_copy(ref, ref, recv_sem.at[phase]).wait()

    def sent(phase, ref):
        pltpu.make_async_copy(ref, ref, send_sem.at[phase]).wait()

    barrier = pltpu.get_barrier_semaphore()

    def greet(t):
        pl.semaphore_signal(barrier, inc=1, device_id=anyone(t), device_id_type=MESH)

    each(1, ROWS * COLS, greet)

    loads[1].wait()
    columns = [tri_in[:, n * 128 : (n + 1) * 128] for n in range(5)]
    turned = [jnp.transpose(block.astype(F32)).astype(BF) for block in columns[:4]]
    weights = jnp.concatenate(
        [
            jnp.concatenate([turned[0], turned[2]], 1),
            jnp.concatenate([turned[1], turned[3]], 1),
        ],
        0,
    )
    lane = lax.broadcasted_iota(jnp.int32, (1, 128), 1)
    row_present = (lax.rem(lane, 64) < lengths[row]).astype(F32)
    col_length = lengths[col // 2] - lax.rem(col, 2) * 32
    zero = jnp.zeros((64, 128), BF)
    loads[0].wait()
    for k in range(32):
        norm = layer_norm(pair[:, k, :], 1).astype(BF)
        twin = jnp.concatenate(
            [jnp.concatenate([norm, zero], 1), jnp.concatenate([zero, norm], 1)], 0
        )
        both = nt(weights, twin)
        mask = row_present * jnp.where(k < col_length, 1.0, 0.0)
        wide[:, k, :] = sigmoid(both[:128]) * both[128:] * mask
    for c in range(0, 128, 16):
        tri_send[c : c + 16] = wide[c : c + 16].astype(BF)

    pl.semaphore_wait(barrier, ROWS * COLS - 1)

    def push_tri(t):
        r, c = anyone(t)
        push(TRI, tri_send.at[r * COLS + c], tri_got.at[me], (r, c), tri_sem.at[row])

    each(1, ROWS * COLS, push_tri)
    tri_got[me] = tri_send[me]

    for k in range(32):
        norm = layer_norm(pair[:, k, :], 1).astype(BF)
        gate[:, k, :] = sigmoid(nn(norm, columns[4]))
    for load in loads[2:]:
        load.wait()
    group = lane_group(128)
    mine_first = jnp.where(core == 0, 1.0, 0.0)
    for t in range(4):
        block = att_in[:, t * 128 : (t + 1) * 128].astype(F32)
        low = jnp.where(group < 2, block, 0.0)
        high = jnp.where(group < 2, 0.0, block)
        low_up, high_down = roll(low, 64), roll(high, 64)
        if t == 3:
            gate_packed[0:128, 0:128] = low.astype(BF)
            gate_packed[128:256, 0:128] = low_up.astype(BF)
            gate_packed[0:128, 128:256] = high_down.astype(BF)
            gate_packed[128:256, 128:256] = high.astype(BF)
        else:
            at = slice(t * 128, t * 128 + 128)
            packed[0:128, at] = jnp.where(mine_first > 0.5, low, high_down).astype(BF)
            packed[128:256, at] = jnp.where(mine_first > 0.5, low_up, high).astype(BF)
    out_packed[...] = jnp.zeros_like(out_packed)
    for p in range(2):
        for i in range(2):
            at = p * 128 + i * 64
            out_packed[at : at + 64, i * 128 : (i + 1) * 128] = att_out[p * 64 : p * 64 + 64, :]
    rest = att_bias[...]
    bias_weights = []
    for _ in range(3):
        part = rest.astype(BF)
        rest = rest - part.astype(F32)
        bias_weights.append(part)

    group = lane_group(16)

    def near(distance):
        return lax.rem(row - distance + ROWS, ROWS)

    def product(r, s):
        full = nn(turned_left[r], tri_got[pl.ds(s * COLS, COLS)].reshape(512, 128))
        parts = [full[g * 16 : (g + 1) * 16] for g in range(4)]
        for half in range(2):
            packed_rows = None
            for g in range(4):
                piece = roll(parts[g], g * 32 - 64 - half * 32)
                packed_rows = piece if g == 0 else jnp.where(group == g, piece, packed_rows)
            back_send[r * COLS + s * 2 + half] = packed_rows.astype(BF)

    def push_back(r, c):
        @pl.when(r * COLS + c != me)
        def _():
            push(BACK, back_send.at[r * COLS + c], back_got.at[me], (r, c))

    for distance in range(ROWS):
        new = near(distance)
        arrived = tri_got.at[pl.ds(0, COLS - 1 if distance == 0 else COLS)]
        pltpu.make_async_copy(arrived, arrived, tri_sem.at[new]).wait()
        got = tri_got[pl.ds(new * COLS, COLS)].reshape(512, 128)
        turned_left[new] = jnp.transpose(got.astype(F32))[:64].astype(BF)
        product(new, new)
        for older in range(distance):
            product(new, near(older))
            product(near(older), new)

        def push_new(older):
            push_back(new, near(older) * 2)
            push_back(new, near(older) * 2 + 1)

        def push_older(older):
            push_back(near(older), new * 2)
            push_back(near(older), new * 2 + 1)

        each(0, distance + 1, push_new)
        each(0, distance, push_older)
    back_got[me] = back_send[me]
    landed(BACK, back_got.at[pl.ds(0, ROWS * COLS - 1)])

    for c in range(0, 128, 16):
        wide[c : c + 16, 0:16] = back_got[c : c + 16].astype(F32)
    for lo in range(16):
        update = tn(layer_norm(wide[:, lo, :], 0).astype(BF), tri_out[...])
        blocks = []
        for hi in range(4):
            i = hi * 16 + lo
            new = pair[i] + gate[i] * update[hi * 32 : (hi + 1) * 32]
            pair1[i] = new
            block = layer_norm(new, 1).astype(BF)
            at = (lo % 2) * 64 + (hi // 2) * 32
            norm_send[lo // 2, at : at + 32, (hi % 2) * 128 : (hi % 2) * 128 + 128] = block
            blocks.append(block)
        stacked = jnp.concatenate(blocks, 0)
        parts = [nt(w, stacked) for w in bias_weights]
        bias = parts[0] + (parts[1] + parts[2])
        for h in range(H):
            bias_send[h, lo : lo + 1, :] = bias[h : h + 1]

    def push_bias_col(t):
        c = lax.rem(col + t, COLS)
        heads = bias_send.at[pl.ds(lax.rem(c, 2) * 2, 2)]
        push(BIAS_COL, heads, bias_got.at[col], (row, c))

    each(1, COLS, push_bias_col)
    bias_got[col] = bias_send[pl.ds(core * 2, 2)]

    def differ(a, b):
        return a + b - 2 * a * b

    chip = col // 2

    def chip_partner(t):
        flip = 8 - t
        low = differ(lax.rem(chip, 2), flip % 2)
        high = differ(lax.rem(chip // 2, 2), flip // 2 % 2)
        return low + 2 * high + 4 * differ(chip // 4, flip // 4)

    def push_norm(t):
        g = chip_partner(t)
        push(NORM, norm_send.at[g], norm_got.at[core, chip], (row, g * 2 + core), norm_sem.at[chip])

    def push_twin(g):
        twin = norm_got.at[core, g]
        push(NORM_TWIN, twin, twin, (row, col + 1 - 2 * core))

    each(1, 8, push_norm)
    norm_got[core, chip] = norm_send[chip]

    landed(BIAS_COL, bias_got.at[pl.ds(0, COLS - 1)])
    for h in range(2):
        for hi in range(4):
            quads = []
            for quad in range(4):
                rows = None
                for q in range(4):
                    piece = roll(bias_got[quad * 4 + q, h], q * 32 - hi * 32)
                    rows = piece if q == 0 else jnp.where(group == q, piece, rows)
                length = jnp.where(lane < 64, lengths[quad * 2], lengths[quad * 2 + 1])
                quads.append(jnp.where(lax.rem(lane, 64) < length, rows, -1000000000.0))
            rows = jnp.concatenate(quads, 1)
            top = jnp.max(rows, axis=1, keepdims=True)
            bias_rows[h, hi * 16 : hi * 16 + 16] = (rows - top).astype(BF)
    bias_all[row] = bias_rows[...]

    def partner(step):
        t = lax.rem(step - 1 + chip, 7) + 1
        flip = 3 - (t - 1) // 2
        low = differ(lax.rem(row, 2), lax.rem(flip, 2))
        high = differ(lax.rem(row // 2, 2), flip // 2)
        return low + 2 * high + 4 * differ(row // 4, 1 - lax.rem(t, 2) + t // 7)

    def push_bias_row(t):
        push(BIAS_ROW, bias_rows, bias_all.at[row], (partner(t), col), row_sem.at[row])

    push_twin(chip)
    each(1, ROWS, push_bias_row)

    for g in range(8):
        gate2[g] = sigmoid(nn(norm_send[g], gate_packed[...]))

    def hand_over(t):
        g = chip_partner(t)
        pltpu.make_async_copy(norm_got.at[0, 0], norm_got.at[0, 0], norm_sem.at[g]).wait()
        push_twin(g)

    each(1, 8, hand_over)
    landed(NORM_TWIN, norm_got.at[0])
    ones = jnp.ones((512, 128), BF)
    for n in range(4):
        normed = jnp.swapaxes(norm_got[:, :, n * 32 : n * 32 + 32, :], 0, 1).reshape(512, 256)
        queries[n] = (nn(normed, packed[:, 0:128]) * (DH ** (-0.5))).astype(BF)
        keys[n] = nn(normed, packed[:, 128:256]).astype(BF)
        values[n, :, 0:128] = nn(normed, packed[:, 256:384]).astype(BF)
        values[n, :, 128:256] = ones

    group = lane_group(64)

    def attend(r):
        at = pl.ds(pl.multiple_of(r * 64, 64), 64)

        def pair_of_rows(n):
            query = queries[n, at, :]
            mine = [jnp.where(group == g, query, jnp.zeros_like(query)) for g in range(4)]
            bias = [bias_all[r, 0].astype(F32), bias_all[r, 1].astype(F32)]
            score = nt(jnp.concatenate(mine, 0), keys[n]) + jnp.concatenate(bias + bias, 0)
            top = jnp.max(score, axis=1, keepdims=True)
            summed = nn(jnp.exp(score - top).astype(BF), values[n])
            result = summed[:, :128] / summed[:, 128:]
            total = result[0:64]
            for g in range(1, 4):
                total = jnp.where(group == g, result[g * 64 : g * 64 + 64], total)
            to = slice(n * 32, n * 32 + 32)
            head_send[2 * r, to, :] = total[:32].astype(BF)
            head_send[2 * r + 1, to, :] = total[32:].astype(BF)

        for n in range(4):
            pair_of_rows(n)
        for c in (2 * r, 2 * r + 1):

            @pl.when(c != col)
            def _():
                push(HEADS, head_send.at[c], head_got.at[col], (row, c))

    attend(row)

    def attend_next(t):
        r = partner(t)
        pltpu.make_async_copy(bias_rows, bias_rows, row_sem.at[r]).wait()
        attend(r)

    each(1, ROWS, attend_next)
    head_got[col] = head_send[col]
    landed(HEADS, head_got.at[pl.ds(0, COLS - 1)])

    for g in range(8):
        heads = jnp.concatenate([head_got[2 * g], head_got[2 * g + 1]], 1).astype(F32)
        result = nn((gate2[g] * heads).astype(BF), out_packed[...])
        for l in range(2):
            for hi in range(4):
                i = hi * 16 + g * 2 + l
                at = l * 64 + (hi // 2) * 32
                lanes = slice((hi % 2) * 128, (hi % 2) * 128 + 128)
                out[i] = pair1[i] + result[at : at + 32, lanes]

    sent(TRI, tri_send.at[pl.ds(0, ROWS * COLS - 1)])
    sent(BACK, back_send.at[pl.ds(0, ROWS * COLS - 1)])
    sent(NORM, norm_got.at[0, pl.ds(0, 7)])
    sent(NORM_TWIN, norm_got.at[0])
    sent(BIAS_COL, bias_got.at[pl.ds(0, COLS - 1)])
    sent(BIAS_ROW, bias_all.at[pl.ds(0, ROWS - 1)])
    sent(HEADS, head_send.at[pl.ds(0, COLS - 1)])


def on_device(pair, chain_lengths, tri_in, tri_out, att_in, att_bias, att_out):
    vmem = pl.BlockSpec(memory_space=pltpu.VMEM)
    return pl.pallas_call(
        block_kernel,
        out_shape=jax.ShapeDtypeStruct((64, 32, 128), F32),
        in_specs=[pl.BlockSpec(memory_space=pltpu.SMEM)] + [pl.BlockSpec(memory_space=pltpu.HBM)] * 6,
        out_specs=vmem,
        scratch_shapes=[
            pltpu.VMEM((64, 32, 128), F32),
            pltpu.VMEM((128, 640), BF),
            pltpu.VMEM((128, 128), BF),
            pltpu.VMEM((128, 512), BF),
            pltpu.VMEM((4, 128), F32),
            pltpu.VMEM((128, 128), BF),
            pltpu.VMEM((128, 32, 128), BF),
            pltpu.VMEM((128, 32, 128), BF),
            pltpu.VMEM((128, 16, 128), BF),
            pltpu.VMEM((128, 16, 128), BF),
            pltpu.VMEM((8, 128, 256), BF),
            pltpu.VMEM((2, 8, 128, 256), BF),
            pltpu.VMEM((4, 16, 128), F32),
            pltpu.VMEM((16, 2, 16, 128), F32),
            pltpu.VMEM((2, 64, 512), BF),
            pltpu.VMEM((8, 2, 64, 512), BF),
            pltpu.VMEM((16, 128, 128), BF),
            pltpu.VMEM((16, 128, 128), BF),
            pltpu.VMEM((8, 64, 512), BF),
            pltpu.VMEM((4, 512, 128), BF),
            pltpu.VMEM((4, 512, 128), BF),
            pltpu.VMEM((4, 512, 256), BF),
            pltpu.VMEM((128, 32, 128), F32),
            pltpu.VMEM((64, 32, 128), F32),
            pltpu.VMEM((8, 128, 256), F32),
            pltpu.VMEM((64, 32, 128), F32),
            pltpu.VMEM((256, 384), BF),
            pltpu.VMEM((256, 256), BF),
            pltpu.VMEM((256, 256), BF),
            pltpu.SemaphoreType.DMA((6,)),
            pltpu.SemaphoreType.DMA((7,)),
            pltpu.SemaphoreType.DMA((7,)),
            pltpu.SemaphoreType.DMA((8,)),
            pltpu.SemaphoreType.DMA((8,)),
            pltpu.SemaphoreType.DMA((8,)),
        ],
        name="pairformer",
        compiler_params=pltpu.CompilerParams(
            collective_id=0, has_side_effects=True, vmem_limit_bytes=63 << 20
        ),
    )(chain_lengths, pair, tri_in, tri_out, att_in, att_bias.T, att_out)


def solution(mesh):
    return jax.shard_map(
        on_device,
        mesh=mesh,
        in_specs=(P("row", "col", None), P(), P(), P(), P(), P(), P()),
        out_specs=P("row", "col", None),
        check_vma=False,
    )
```

```python
import jax
import jax.numpy as jnp
from jax import lax
from jax.experimental import pallas as pl
from jax.experimental.pallas import tpu as pltpu
from jax.sharding import PartitionSpec as P

MESH = pl.DeviceIdType.MESH
H = 4
DH = 32
ROWS = 8
COLS = 16
BF = jnp.bfloat16
F32 = jnp.float32
TRI, BACK, NORM, NORM_TWIN, BIAS_COL, BIAS_ROW, HEADS = range(7)


def layer_norm(values, axis):
    center = values - jnp.mean(values, axis=axis, keepdims=True)
    spread = jnp.mean(center * center, axis=axis, keepdims=True)
    return center * lax.rsqrt(spread + 1e-05)


def nt(a, b):
    return lax.dot_general(a, b, (((1,), (1,)), ((), ())), preferred_element_type=F32)


def tn(a, b):
    return lax.dot_general(a, b, (((0,), (0,)), ((), ())), preferred_element_type=F32)


def nn(a, b):
    return lax.dot_general(a, b, (((1,), (0,)), ((), ())), preferred_element_type=F32)


def sigmoid(x):
    return 1.0 / (1.0 + jnp.exp(-x))


def lane_group(rows):
    return lax.broadcasted_iota(jnp.int32, (rows, 128), 1) // 32


def roll(x, shift):
    return x if shift % 128 == 0 else pltpu.roll(x, shift % 128, 1)


def block_kernel(
    lengths, pair_in, tri_in_in, tri_out_in, att_in_in, att_bias_in, att_out_in, out,
    pair, tri_in, tri_out, att_in, att_bias, att_out,
    tri_send, tri_got, back_send, back_got, norm_send, norm_got,
    bias_send, bias_got, bias_rows, bias_all, head_send, head_got,
    turned_left, queries, keys, values, wide, gate, gate2, pair1, packed, gate_packed, out_packed, load_sem, send_sem, recv_sem, tri_sem, norm_sem, row_sem,
):
    row, col = lax.axis_index("row"), lax.axis_index("col")
    me = row * COLS + col
    core = lax.rem(col, 2)

    loads = [
        pltpu.make_async_copy(src, dst, load_sem.at[n])
        for n, (src, dst) in enumerate(
            [
                (pair_in, pair), (tri_in_in, tri_in), (att_in_in, att_in),
                (att_out_in, att_out), (att_bias_in, att_bias), (tri_out_in, tri_out),
            ]
        )
    ]
    for load in loads:
        load.start()

    def anyone(t):
        return lax.rem(row + t // COLS, ROWS), lax.rem(col + lax.rem(t, COLS), COLS)

    def each(start, stop, body):
        def step(t, carry):
            body(t)
            return carry

        lax.fori_loop(start, stop, step, 0)

    def push(phase, src, dst, device, arrival=None):
        pltpu.make_async_remote_copy(
            src_ref=src, dst_ref=dst, send_sem=send_sem.at[phase],
            recv_sem=recv_sem.at[phase] if arrival is None else arrival,
            device_id=device, device_id_type=MESH,
        ).start()

    def landed(phase, ref):
        pltpu.make_async_copy(ref, ref, recv_sem.at[phase]).wait()

    def sent(phase, ref):
        pltpu.make_async_copy(ref, ref, send_sem.at[phase]).wait()

    barrier = pltpu.get_barrier_semaphore()

    def greet(t):
        pl.semaphore_signal(barrier, inc=1, device_id=anyone(t), device_id_type=MESH)

    each(1, ROWS * COLS, greet)

    loads[1].wait()
    columns = [tri_in[:, n * 128 : (n + 1) * 128] for n in range(5)]
    turned = [jnp.transpose(block.astype(F32)).astype(BF) for block in columns[:4]]
    weights = jnp.concatenate(
        [
            jnp.concatenate([turned[0], turned[2]], 1),
            jnp.concatenate([turned[1], turned[3]], 1),
        ],
        0,
    )
    lane = lax.broadcasted_iota(jnp.int32, (1, 128), 1)
    row_present = (lax.rem(lane, 64) < lengths[row]).astype(F32)
    col_length = lengths[col // 2] - lax.rem(col, 2) * 32
    zero = jnp.zeros((64, 128), BF)
    loads[0].wait()
    for k in range(32):
        norm = layer_norm(pair[:, k, :], 1).astype(BF)
        twin = jnp.concatenate(
            [jnp.concatenate([norm, zero], 1), jnp.concatenate([zero, norm], 1)], 0
        )
        both = nt(weights, twin)
        mask = row_present * jnp.where(k < col_length, 1.0, 0.0)
        wide[:, k, :] = sigmoid(both[:128]) * both[128:] * mask
    for c in range(0, 128, 16):
        tri_send[c : c + 16] = wide[c : c + 16].astype(BF)

    pl.semaphore_wait(barrier, ROWS * COLS - 1)

    def push_tri(t):
        r, c = anyone(t)
        push(TRI, tri_send.at[r * COLS + c], tri_got.at[me], (r, c), tri_sem.at[row])

    each(1, ROWS * COLS, push_tri)
    tri_got[me] = tri_send[me]

    for k in range(32):
        norm = layer_norm(pair[:, k, :], 1).astype(BF)
        gate[:, k, :] = sigmoid(nn(norm, columns[4]))
    for load in loads[2:]:
        load.wait()
    group = lane_group(128)
    mine_first = jnp.where(core == 0, 1.0, 0.0)
    for t in range(4):
        block = att_in[:, t * 128 : (t + 1) * 128].astype(F32)
        low = jnp.where(group < 2, block, 0.0)
        high = jnp.where(group < 2, 0.0, block)
        low_up, high_down = roll(low, 64), roll(high, 64)
        if t == 3:
            gate_packed[0:128, 0:128] = low.astype(BF)
            gate_packed[128:256, 0:128] = low_up.astype(BF)
            gate_packed[0:128, 128:256] = high_down.astype(BF)
            gate_packed[128:256, 128:256] = high.astype(BF)
        else:
            at = slice(t * 128, t * 128 + 128)
            packed[0:128, at] = jnp.where(mine_first > 0.5, low, high_down).astype(BF)
            packed[128:256, at] = jnp.where(mine_first > 0.5, low_up, high).astype(BF)
    out_packed[...] = jnp.zeros_like(out_packed)
    for p in range(2):
        for i in range(2):
            at = p * 128 + i * 64
            out_packed[at : at + 64, i * 128 : (i + 1) * 128] = att_out[p * 64 : p * 64 + 64, :]
    rest = att_bias[...]
    bias_weights = []
    for _ in range(3):
        part = rest.astype(BF)
        rest = rest - part.astype(F32)
        bias_weights += [part.astype(F32), jnp.zeros((4, 128), F32)]

    bias_weights = jnp.concatenate(bias_weights, 0).astype(BF)

    group = lane_group(16)

    def near(distance):
        return lax.rem(row - distance + ROWS, ROWS)

    def product(r, s):
        full = nn(turned_left[r], tri_got[pl.ds(s * COLS, COLS)].reshape(512, 128))
        parts = [full[g * 16 : (g + 1) * 16] for g in range(4)]
        for half in range(2):
            packed_rows = None
            for g in range(4):
                piece = roll(parts[g], g * 32 - 64 - half * 32)
                packed_rows = piece if g == 0 else jnp.where(group == g, piece, packed_rows)
            back_send[r * COLS + s * 2 + half] = packed_rows.astype(BF)

    def push_back(r, c):
        @pl.when(r * COLS + c != me)
        def _():
            push(BACK, back_send.at[r * COLS + c], back_got.at[me], (r, c))

    for distance in range(ROWS):
        new = near(distance)
        arrived = tri_got.at[pl.ds(0, COLS - 1 if distance == 0 else COLS)]
        pltpu.make_async_copy(arrived, arrived, tri_sem.at[new]).wait()
        got = tri_got[pl.ds(new * COLS, COLS)].reshape(512, 128)
        turned_left[new] = jnp.transpose(got.astype(F32))[:64].astype(BF)
        product(new, new)
        for older in range(distance):
            product(new, near(older))
            product(near(older), new)

        def push_new(older):
            push_back(new, near(older) * 2)
            push_back(new, near(older) * 2 + 1)

        def push_older(older):
            push_back(near(older), new * 2)
            push_back(near(older), new * 2 + 1)

        each(0, distance + 1, push_new)
        each(0, distance, push_older)
    back_got[me] = back_send[me]
    landed(BACK, back_got.at[pl.ds(0, ROWS * COLS - 1)])

    for c in range(0, 128, 16):
        wide[c : c + 16, 0:16] = back_got[c : c + 16].astype(F32)
    for lo in range(16):
        update = tn(layer_norm(wide[:, lo, :], 0).astype(BF), tri_out[...])
        blocks = []
        for hi in range(4):
            i = hi * 16 + lo
            new = pair[i] + gate[i] * update[hi * 32 : (hi + 1) * 32]
            pair1[i] = new
            block = layer_norm(new, 1).astype(BF)
            at = (lo % 2) * 64 + (hi // 2) * 32
            norm_send[lo // 2, at : at + 32, (hi % 2) * 128 : (hi % 2) * 128 + 128] = block
            blocks.append(block)
        stacked = jnp.concatenate(blocks, 0)
        parts = nt(bias_weights, stacked)
        bias = parts[0:4] + (parts[8:12] + parts[16:20])
        for h in range(H):
            bias_send[h, lo : lo + 1, :] = bias[h : h + 1]

    def push_bias_col(t):
        c = lax.rem(col + t, COLS)
        heads = bias_send.at[pl.ds(lax.rem(c, 2) * 2, 2)]
        push(BIAS_COL, heads, bias_got.at[col], (row, c))

    each(1, COLS, push_bias_col)
    bias_got[col] = bias_send[pl.ds(core * 2, 2)]

    def differ(a, b):
        return a + b - 2 * a * b

    chip = col // 2

    def chip_partner(t):
        flip = 8 - t
        low = differ(lax.rem(chip, 2), flip % 2)
        high = differ(lax.rem(chip // 2, 2), flip // 2 % 2)
        return low + 2 * high + 4 * differ(chip // 4, flip // 4)

    def push_norm(t):
        g = chip_partner(t)
        push(NORM, norm_send.at[g], norm_got.at[core, chip], (row, g * 2 + core), norm_sem.at[chip])

    def push_twin(g):
        twin = norm_got.at[core, g]
        push(NORM_TWIN, twin, twin, (row, col + 1 - 2 * core))

    each(1, 8, push_norm)
    norm_got[core, chip] = norm_send[chip]

    landed(BIAS_COL, bias_got.at[pl.ds(0, COLS - 1)])
    for h in range(2):
        for hi in range(4):
            quads = []
            for quad in range(4):
                rows = None
                for q in range(4):
                    piece = roll(bias_got[quad * 4 + q, h], q * 32 - hi * 32)
                    rows = piece if q == 0 else jnp.where(group == q, piece, rows)
                length = jnp.where(lane < 64, lengths[quad * 2], lengths[quad * 2 + 1])
                quads.append(jnp.where(lax.rem(lane, 64) < length, rows, -1000000000.0))
            rows = jnp.concatenate(quads, 1)
            top = jnp.max(rows, axis=1, keepdims=True)
            bias_rows[h, hi * 16 : hi * 16 + 16] = (rows - top).astype(BF)
    bias_all[row] = bias_rows[...]

    def partner(step):
        t = lax.rem(step - 1 + chip, 7) + 1
        flip = 3 - (t - 1) // 2
        low = differ(lax.rem(row, 2), lax.rem(flip, 2))
        high = differ(lax.rem(row // 2, 2), flip // 2)
        return low + 2 * high + 4 * differ(row // 4, 1 - lax.rem(t, 2) + t // 7)

    def push_bias_row(t):
        push(BIAS_ROW, bias_rows, bias_all.at[row], (partner(t), col), row_sem.at[row])

    push_twin(chip)
    each(1, ROWS, push_bias_row)

    for g in range(8):
        gate2[g] = sigmoid(nn(norm_send[g], gate_packed[...]))

    def hand_over(t):
        g = chip_partner(t)
        pltpu.make_async_copy(norm_got.at[0, 0], norm_got.at[0, 0], norm_sem.at[g]).wait()
        push_twin(g)

    each(1, 8, hand_over)
    landed(NORM_TWIN, norm_got.at[0])
    ones = jnp.ones((512, 128), BF)
    for n in range(4):
        normed = jnp.swapaxes(norm_got[:, :, n * 32 : n * 32 + 32, :], 0, 1).reshape(512, 256)
        queries[n] = (nn(normed, packed[:, 0:128]) * (DH ** (-0.5))).astype(BF)
        keys[n] = nn(normed, packed[:, 128:256]).astype(BF)
        values[n, :, 0:128] = nn(normed, packed[:, 256:384]).astype(BF)
        values[n, :, 128:256] = ones

    group = lane_group(64)

    def attend(r):
        at = pl.ds(pl.multiple_of(r * 64, 64), 64)

        def pair_of_rows(n):
            query = queries[n, at, :]
            mine = [jnp.where(group == g, query, jnp.zeros_like(query)) for g in range(4)]
            bias = [bias_all[r, 0].astype(F32), bias_all[r, 1].astype(F32)]
            score = nt(jnp.concatenate(mine, 0), keys[n]) + jnp.concatenate(bias + bias, 0)
            top = jnp.max(score, axis=1, keepdims=True)
            summed = nn(jnp.exp(score - top).astype(BF), values[n])
            result = summed[:, :128] / summed[:, 128:]
            total = result[0:64]
            for g in range(1, 4):
                total = jnp.where(group == g, result[g * 64 : g * 64 + 64], total)
            to = slice(n * 32, n * 32 + 32)
            head_send[2 * r, to, :] = total[:32].astype(BF)
            head_send[2 * r + 1, to, :] = total[32:].astype(BF)

        for n in range(4):
            pair_of_rows(n)
        for c in (2 * r, 2 * r + 1):

            @pl.when(c != col)
            def _():
                push(HEADS, head_send.at[c], head_got.at[col], (row, c))

    attend(row)

    def attend_next(t):
        r = partner(t)
        pltpu.make_async_copy(bias_rows, bias_rows, row_sem.at[r]).wait()
        attend(r)

    each(1, ROWS, attend_next)
    head_got[col] = head_send[col]
    landed(HEADS, head_got.at[pl.ds(0, COLS - 1)])

    for g in range(8):
        heads = jnp.concatenate([head_got[2 * g], head_got[2 * g + 1]], 1).astype(F32)
        result = nn((gate2[g] * heads).astype(BF), out_packed[...])
        for l in range(2):
            for hi in range(4):
                i = hi * 16 + g * 2 + l
                at = l * 64 + (hi // 2) * 32
                lanes = slice((hi % 2) * 128, (hi % 2) * 128 + 128)
                out[i] = pair1[i] + result[at : at + 32, lanes]

    sent(TRI, tri_send.at[pl.ds(0, ROWS * COLS - 1)])
    sent(BACK, back_send.at[pl.ds(0, ROWS * COLS - 1)])
    sent(NORM, norm_got.at[0, pl.ds(0, 7)])
    sent(NORM_TWIN, norm_got.at[0])
    sent(BIAS_COL, bias_got.at[pl.ds(0, COLS - 1)])
    sent(BIAS_ROW, bias_all.at[pl.ds(0, ROWS - 1)])
    sent(HEADS, head_send.at[pl.ds(0, COLS - 1)])


def on_device(pair, chain_lengths, tri_in, tri_out, att_in, att_bias, att_out):
    vmem = pl.BlockSpec(memory_space=pltpu.VMEM)
    return pl.pallas_call(
        block_kernel,
        out_shape=jax.ShapeDtypeStruct((64, 32, 128), F32),
        in_specs=[pl.BlockSpec(memory_space=pltpu.SMEM)] + [pl.BlockSpec(memory_space=pltpu.HBM)] * 6,
        out_specs=vmem,
        scratch_shapes=[
            pltpu.VMEM((64, 32, 128), F32),
            pltpu.VMEM((128, 640), BF),
            pltpu.VMEM((128, 128), BF),
            pltpu.VMEM((128, 512), BF),
            pltpu.VMEM((4, 128), F32),
            pltpu.VMEM((128, 128), BF),
            pltpu.VMEM((128, 32, 128), BF),
            pltpu.VMEM((128, 32, 128), BF),
            pltpu.VMEM((128, 16, 128), BF),
            pltpu.VMEM((128, 16, 128), BF),
            pltpu.VMEM((8, 128, 256), BF),
            pltpu.VMEM((2, 8, 128, 256), BF),
            pltpu.VMEM((4, 16, 128), F32),
            pltpu.VMEM((16, 2, 16, 128), F32),
            pltpu.VMEM((2, 64, 512), BF),
            pltpu.VMEM((8, 2, 64, 512), BF),
            pltpu.VMEM((16, 128, 128), BF),
            pltpu.VMEM((16, 128, 128), BF),
            pltpu.VMEM((8, 64, 512), BF),
            pltpu.VMEM((4, 512, 128), BF),
            pltpu.VMEM((4, 512, 128), BF),
            pltpu.VMEM((4, 512, 256), BF),
            pltpu.VMEM((128, 32, 128), F32),
            pltpu.VMEM((64, 32, 128), F32),
            pltpu.VMEM((8, 128, 256), F32),
            pltpu.VMEM((64, 32, 128), F32),
            pltpu.VMEM((256, 384), BF),
            pltpu.VMEM((256, 256), BF),
            pltpu.VMEM((256, 256), BF),
            pltpu.SemaphoreType.DMA((6,)),
            pltpu.SemaphoreType.DMA((7,)),
            pltpu.SemaphoreType.DMA((7,)),
            pltpu.SemaphoreType.DMA((8,)),
            pltpu.SemaphoreType.DMA((8,)),
            pltpu.SemaphoreType.DMA((8,)),
        ],
        name="pairformer",
        compiler_params=pltpu.CompilerParams(
            collective_id=0, has_side_effects=True, vmem_limit_bytes=63 << 20
        ),
    )(chain_lengths, pair, tri_in, tri_out, att_in, att_bias.T, att_out)


def solution(mesh):
    return jax.shard_map(
        on_device,
        mesh=mesh,
        in_specs=(P("row", "col", None), P(), P(), P(), P(), P(), P()),
        out_specs=P("row", "col", None),
        check_vma=False,
    )
```
